256 devices in a mesh: slot: 16 (over z, core), param: 16 (over x, y).
Axes of the slice: x: 4, y: 4, z: 8, core: 2. Of those that a mesh axis runs over, the one named last changes fastest.
Arguments:
- step_hist: float32 [16, 2097152], P('slot', 'param'), may hold values from -22 to 22
- diff_hist: float32 [16, 2097152], P('slot', 'param'), may hold values from -61 to 61
- gradient: float32 [2097152], P('param'), may hold values from -11 to 11
Outputs:
- direction: float32 [2097152], P('param')
- gram_matrix: float32 [33, 33], replicated
The draws below stay inside these ranges and needn't reach their ends.
All inputs are finite; a program needn't handle non-finite values.
Results may differ from the reference program's by a relative error of at most 0.0003.
Values may be sent and summed in bfloat16 or wider, within the bound.
A program may use at most 320 MiB of HBM per device.

```python
import math
import jax
import jax.numpy as jnp
from jax import lax

HIST = 16
P_SIZE = 2097152


def ramp_scale(count):
    position = jnp.arange(count, dtype=jnp.float32) / count
    return 0.6 * jnp.exp(math.log(3.0) * position)


def mixed_base(key):
    keys = jax.random.split(key, 3)
    normal_part = jnp.clip(jax.random.normal(keys[0], (HIST, P_SIZE), jnp.float32), -6.0, 6.0)
    base = normal_part
    mixing = jnp.clip(jax.random.normal(keys[2], (HIST, HIST), jnp.float32), -3.0, 3.0) * (0.3 / math.sqrt(HIST))
    mixing = mixing + jnp.eye(HIST, dtype=jnp.float32)
    mixed = mixing[:, 0:1] * base[0:1, :]
    for index in range(1, HIST):
        mixed = mixed + mixing[:, index:index + 1] * base[index:index + 1, :]
    return jnp.clip(mixed, -6.0, 6.0)


def history_pairs(key):
    mixed = mixed_base(key)
    keys = jax.random.split(jax.random.fold_in(key, 11), 3)
    slot_scale = jnp.exp(jax.random.uniform(keys[0], (HIST, 1), jnp.float32, math.log(0.5), math.log(2.0)))
    curvature = jnp.exp(jax.random.uniform(keys[1], (HIST, P_SIZE), jnp.float32, math.log(0.5), math.log(2.5)))
    jitter = jax.random.uniform(keys[2], (HIST, P_SIZE), jnp.float32, -1.0, 1.0)
    steps = mixed * slot_scale * ramp_scale(P_SIZE)[None, :]
    diffs = (curvature + 0.25 * jitter) * steps
    return (steps, diffs)


def draw_step_hist(key, part):
    steps, diffs = history_pairs(key)
    return steps


def draw_diff_hist(key, part):
    steps, diffs = history_pairs(key)
    return diffs


def draw_gradient(key, part):
    shared = mixed_base(key)
    key = jax.random.fold_in(key, 7)
    keys = jax.random.split(key, 2)
    own = jnp.clip(jax.random.normal(keys[0], (P_SIZE,), jnp.float32), -6.0, 6.0)
    weights = jnp.clip(jax.random.normal(keys[1], (HIST, 1), jnp.float32), -3.0, 3.0) * (0.5 / math.sqrt(HIST))
    combined = jnp.clip(own + jnp.sum(weights * shared, axis=0), -6.0, 6.0)
    return combined * ramp_scale(P_SIZE)


def setup_inputs(seed: int = 0) -> dict:
    seeds = jax.random.split(jax.random.key(seed), 4)
    return {
        "step_hist": draw_step_hist(jax.random.fold_in(seeds[3], 71), 0),
        "diff_hist": draw_diff_hist(jax.random.fold_in(seeds[3], 71), 0),
        "gradient": draw_gradient(jax.random.fold_in(seeds[3], 71), 0),
    }


def coefficients(gram_matrix):
    history = (gram_matrix.shape[0] - 1) // 2
    coeffs = jnp.zeros((2 * history + 1,), jnp.float32).at[2 * history].set(-1.0)
    alphas = [None] * history
    inverses = [None] * history
    for position in reversed(range(history)):
        inverse = 1.0 / gram_matrix[position, history + position]
        alpha_term = inverse * jnp.sum(coeffs * gram_matrix[:, position])
        coeffs = coeffs.at[history + position].add(-alpha_term)
        alphas[position] = alpha_term
        inverses[position] = inverse
    coeffs = coeffs * (gram_matrix[history - 1, 2 * history - 1] / gram_matrix[2 * history - 1, 2 * history - 1])
    for position in range(history):
        beta_term = inverses[position] * jnp.sum(coeffs * gram_matrix[history + position, :])
        coeffs = coeffs.at[position].add(alphas[position] - beta_term)
    return coeffs


def reference(step_hist, diff_hist, gradient):
    vectors = jnp.concatenate([step_hist, diff_hist, gradient[None, :]], axis=0)
    lowered = vectors.astype(jnp.bfloat16)
    gram_matrix = jnp.dot(lowered, lowered.T, preferred_element_type=jnp.float32) / P_SIZE
    coeffs = coefficients(gram_matrix)
    direction = jnp.dot(coeffs, vectors, precision=lax.Precision.HIGHEST, preferred_element_type=jnp.float32)
    return direction, gram_matrix
```

```python
import functools

import jax
import jax.numpy as jnp
from jax import lax
from jax.experimental import pallas as pl
from jax.experimental.pallas import tpu as pltpu
from jax.sharding import PartitionSpec as P

HIST = 16
SLOTS = 16
COLS = 16
ROWS = 1024
PIECE = ROWS // SLOTS
VECS = 40
LANES = 128
STRIDE = PIECE
F32, BF16 = jnp.float32, jnp.bfloat16
MESH = pl.DeviceIdType.MESH
STARTS = (0, 40, 72, 96, 112)


def lanes_between(low, high):
    lane = lax.broadcasted_iota(jnp.int32, (8, LANES), 1)
    return jnp.logical_and(lane >= low, lane < high)


def pack(matrix):
    packed = jnp.zeros((8, LANES), F32)
    for block in range(5):
        rows = matrix[8 * block : 8 * block + 8, :]
        shift = STARTS[block] - 8 * block
        if shift:
            rows = pltpu.roll(rows, shift, 1)
        packed = jnp.where(lanes_between(STARTS[block], STARTS[block] + 40 - 8 * block), rows, packed)
    return packed


def unpack(packed):
    blocks = []
    for block in range(5):
        shift = STARTS[block] - 8 * block
        rows = pltpu.roll(packed, LANES - shift, 1) if shift else packed
        blocks.append(jnp.where(lanes_between(8 * block, 40), rows, 0.0))
    upper = jnp.concatenate(blocks, axis=0)
    lower = jnp.transpose(upper)[:VECS, :]
    lower = jnp.concatenate([lower, jnp.zeros((VECS, LANES - VECS), F32)], axis=1)
    row = lax.broadcasted_iota(jnp.int32, (VECS, LANES), 0)
    col = lax.broadcasted_iota(jnp.int32, (VECS, LANES), 1)
    return jnp.where(col // 8 >= row // 8, upper, lower)


def recursion(gram):
    row = lax.broadcasted_iota(jnp.int32, (VECS, LANES), 0)
    col = lax.broadcasted_iota(jnp.int32, (VECS, LANES), 1)

    def column(j):
        return jnp.broadcast_to(gram[:, j : j + 1], (VECS, LANES))

    def spread(value, i):
        return jnp.broadcast_to(value[i : i + 1, :], (8, LANES))

    def tall(tile):
        return jnp.concatenate([tile] * (VECS // 8), axis=0)

    pairs = jnp.sum(jnp.where(col == row + HIST, gram, 0.0), axis=1, keepdims=True)
    inverses = 1.0 / jnp.broadcast_to(pairs, (VECS, LANES))
    inverse = [spread(inverses, i) for i in range(HIST)]
    products = -column(2 * HIST)
    alphas, steps, diffs = [None] * HIST, [None] * HIST, [None] * HIST
    for i in reversed(range(HIST)):
        alphas[i] = inverse[i] * spread(products, i)
        products = products - tall(alphas[i]) * column(HIST + i)
    scale = spread(column(2 * HIST - 1), HIST - 1) / spread(column(2 * HIST - 1), 2 * HIST - 1)
    products = products * tall(scale)
    for i in range(HIST):
        steps[i] = alphas[i] - inverse[i] * spread(products, HIST + i)
        products = products + tall(steps[i]) * column(i)
        diffs[i] = -alphas[i] * scale
    return steps, diffs, -scale


def kernel(
    step_hbm, diff_hbm, grad_hbm, out_ref, gram_ref,
    step_v, diff_v, grad_v, hi_send, lo_send, hi_recv, lo_recv, wide, square, part, slot_parts, col_parts,
    load_sem, hi_ss, hi_rs, lo_ss, lo_rs, slot_ss, slot_rs, col_ss, col_rs, dir_ss, dir_rs, sib_ss, sib_rs,
):
    me = lax.axis_index("slot")
    col = lax.axis_index("param")
    mate = me + 1 - 2 * lax.rem(me, 2)
    own_rows = pl.ds(pl.multiple_of(me * PIECE, PIECE), PIECE)

    loads = [
        pltpu.make_async_copy(step_hbm, step_v, load_sem.at[0]),
        pltpu.make_async_copy(diff_hbm, diff_v, load_sem.at[1]),
        pltpu.make_async_copy(grad_hbm.at[own_rows], grad_v, load_sem.at[2]),
    ]
    for load in loads:
        load.start()

    barrier = pltpu.get_barrier_semaphore()
    for d in range(1, SLOTS):
        pl.semaphore_signal(barrier, inc=1, device_id={"slot": lax.rem(me + d, SLOTS)}, device_id_type=MESH)
    for d in range(1, COLS):
        pl.semaphore_signal(barrier, inc=1, device_id={"param": lax.rem(col + d, COLS)}, device_id_type=MESH)
    for load in loads:
        load.wait()
    pl.semaphore_wait(barrier, SLOTS + COLS - 2)

    def halves(dest):
        rows = pl.ds(pl.multiple_of(dest * PIECE, PIECE), PIECE)
        return step_v[rows, :], diff_v[rows, :]

    hi_copies = []
    for d in range(1, SLOTS):
        dest = lax.rem(me + d, SLOTS)
        s, y = halves(dest)
        hi_send[dest, :PIECE, :] = s.astype(BF16)
        hi_send[dest, PIECE:, :] = y.astype(BF16)
        copy = pltpu.make_async_remote_copy(
            hi_send.at[dest], hi_recv.at[me], hi_ss.at[d], hi_rs.at[d], device_id={"slot": dest}, device_id_type=MESH
        )
        copy.start()
        hi_copies.append(copy)
    s, y = halves(me)
    hi_recv[me, :PIECE, :] = s.astype(BF16)
    hi_recv[me, PIECE:, :] = y.astype(BF16)

    for k in range(SLOTS):
        for half, source in ((0, step_v), (PIECE, diff_v)):
            v = source[k * PIECE : (k + 1) * PIECE, :]
            lo_send[k, half : half + PIECE, :] = (v - v.astype(BF16).astype(F32)).astype(BF16)
    lo_recv[me] = lo_send[me]

    wide[2 * HIST * STRIDE : 2 * HIST * STRIDE + PIECE, :] = grad_v[...].astype(BF16).astype(F32)
    for j in range(2 * HIST + 1, VECS):
        wide[j * STRIDE : j * STRIDE + PIECE, :] = jnp.zeros((PIECE, LANES), F32)

    for copy in hi_copies:
        copy.wait_recv()

    for k in range(SLOTS):
        wide[k * STRIDE : k * STRIDE + PIECE, :] = hi_recv[k, :PIECE, :].astype(F32)
        wide[(HIST + k) * STRIDE : (HIST + k) * STRIDE + PIECE, :] = hi_recv[k, PIECE:, :].astype(F32)
    rows = [wide[pl.ds(r, VECS, stride=STRIDE), :].astype(BF16) for r in range(PIECE)]
    flat = jnp.concatenate(rows, axis=1)
    square[...] = jnp.zeros((VECS, LANES), F32)
    square[:, :VECS] = lax.dot_general(flat, flat, (((1,), (1,)), ((), ())), preferred_element_type=F32)
    packed = pack(square[...])
    part[0] = packed
    slot_parts[me] = packed
    slot_copies = []
    for d in range(1, SLOTS):
        dest = lax.rem(me + d, SLOTS)
        copy = pltpu.make_async_remote_copy(
            part.at[0], slot_parts.at[me], slot_ss.at[d], slot_rs.at[d], device_id={"slot": dest}, device_id_type=MESH
        )
        copy.start()
        slot_copies.append(copy)

    lo_copies = []
    for d in range(1, SLOTS):
        dest = lax.rem(me + d, SLOTS)
        copy = pltpu.make_async_remote_copy(
            lo_send.at[dest], lo_recv.at[me], lo_ss.at[d], lo_rs.at[d], device_id={"slot": dest}, device_id_type=MESH
        )
        copy.start()
        lo_copies.append(copy)

    for copy in slot_copies:
        copy.wait_recv()
    total = slot_parts[0]
    for k in range(1, SLOTS):
        total = total + slot_parts[k]
    part[1] = total
    col_parts[col] = total
    col_copies = []
    for d in range(1, COLS):
        dest = lax.rem(col + d, COLS)
        copy = pltpu.make_async_remote_copy(
            part.at[1], col_parts.at[col], col_ss.at[d], col_rs.at[d], device_id={"param": dest}, device_id_type=MESH
        )
        copy.start()
        col_copies.append(copy)
    for copy in col_copies:
        copy.wait_recv()
    total = col_parts[0]
    for k in range(1, COLS):
        total = total + col_parts[k]
    gram = unpack(total * (1.0 / (ROWS * LANES * COLS)))
    gram_ref[...] = gram[: 2 * HIST + 1, : 2 * HIST + 1]
    steps, diffs, grad_coeff = recursion(gram)

    for copy in lo_copies:
        copy.wait_recv()
    for t in range(PIECE // 8):
        low, high = 8 * t, 8 * t + 8
        acc = grad_coeff * grad_v[low:high, :]
        for k in range(SLOTS):
            s = hi_recv[k, low:high, :].astype(F32) + lo_recv[k, low:high, :].astype(F32)
            y = hi_recv[k, PIECE + low : PIECE + high, :].astype(F32) + lo_recv[k, PIECE + low : PIECE + high, :].astype(F32)
            acc = acc + steps[k] * s + diffs[k] * y
        out_ref[pl.ds(pl.multiple_of(me * PIECE + low, 8), 8), :] = acc

    chips = SLOTS // 2

    def piece(slot):
        return out_ref.at[pl.ds(pl.multiple_of(slot * PIECE, PIECE), PIECE)]

    dir_copies = {}
    for d in (4, 3, 5, 2, 6, 1, 7):
        dest = lax.rem(me + 2 * d, SLOTS)
        copy = pltpu.make_async_remote_copy(
            piece(me), piece(me), dir_ss.at[d], dir_rs.at[d], device_id={"slot": dest}, device_id_type=MESH
        )
        copy.start()
        dir_copies[d] = copy
    sib_copies = []
    for d in (0, 1, 7, 2, 6, 3, 5, 4):
        if d:
            dir_copies[d].wait_recv()
        source = lax.rem(me + 2 * (chips - d), SLOTS)
        copy = pltpu.make_async_remote_copy(
            piece(source), piece(source), sib_ss.at[d], sib_rs.at[d], device_id={"slot": mate}, device_id_type=MESH
        )
        copy.start()
        sib_copies.append(copy)
    for copy in sib_copies:
        copy.wait_recv()
    for copy in hi_copies + slot_copies + lo_copies + col_copies + list(dir_copies.values()) + sib_copies:
        copy.wait_send()


def call(step, diff, grad):
    dma = pltpu.SemaphoreType.DMA
    return pl.pallas_call(
        kernel,
        out_shape=(
            jax.ShapeDtypeStruct((ROWS, LANES), F32),
            jax.ShapeDtypeStruct((2 * HIST + 1, 2 * HIST + 1), F32),
        ),
        in_specs=[pl.BlockSpec(memory_space=pl.ANY)] * 3,
        out_specs=(pl.BlockSpec(memory_space=pltpu.VMEM), pl.BlockSpec(memory_space=pltpu.VMEM)),
        scratch_shapes=[
            pltpu.VMEM((ROWS, LANES), F32),
            pltpu.VMEM((ROWS, LANES), F32),
            pltpu.VMEM((PIECE, LANES), F32),
            pltpu.VMEM((SLOTS, 2 * PIECE, LANES), BF16),
            pltpu.VMEM((SLOTS, 2 * PIECE, LANES), BF16),
            pltpu.VMEM((SLOTS, 2 * PIECE, LANES), BF16),
            pltpu.VMEM((SLOTS, 2 * PIECE, LANES), BF16),
            pltpu.VMEM((VECS * STRIDE, LANES), F32),
            pltpu.VMEM((VECS, LANES), F32),
            pltpu.VMEM((2, 8, LANES), F32),
            pltpu.VMEM((SLOTS, 8, LANES), F32),
            pltpu.VMEM((COLS, 8, LANES), F32),
            dma((3,)),
            *[dma((SLOTS,))] * 8,
            *[dma((SLOTS // 2,))] * 4,
        ],
        compiler_params=pltpu.CompilerParams(
            collective_id=0, has_side_effects=True, vmem_limit_bytes=60 * 2**20
        ),
        name="lbfgs",
    )(step, diff, grad)


def shards(step_hist, diff_hist, gradient):
    shape = (ROWS, LANES)
    direction, gram = call(step_hist.reshape(shape), diff_hist.reshape(shape), gradient.reshape(shape))
    return direction.reshape(ROWS * LANES), gram


def solution(mesh):
    in_specs = (P("slot", "param"), P("slot", "param"), P("param"))
    out_specs = (P("param"), P())
    return jax.shard_map(shards, mesh=mesh, in_specs=in_specs, out_specs=out_specs, check_vma=False)
```

```python
import functools

import jax
import jax.numpy as jnp
from jax import lax
from jax.experimental import pallas as pl
from jax.experimental.pallas import tpu as pltpu
from jax.sharding import PartitionSpec as P

HIST = 16
SLOTS = 16
COLS = 16
ROWS = 1024
PIECE = ROWS // SLOTS
VECS = 40
LANES = 128
STRIDE = 72
F32, BF16 = jnp.float32, jnp.bfloat16
MESH = pl.DeviceIdType.MESH
SIDE = 4
CHIPS = SLOTS // 2
VMEM_LIMIT = 56 * 2**20
HI_DRAIN = True
LOADS_FIRST = 4
RING_FIRST = True
CORES_IN_PLANE = False
TILE = 16
HI_PARTS = 1
SPAN = PIECE // HI_PARTS
CUTS = (0, 16, 64)
LO_EARLY = 1
PARTS = len(CUTS) - 1
HOPS = (4, 3, 5, 2, 6, 1, 7, 0)
RING = [(dz, flip) for dz in HOPS for flip in (0, 1) if dz or flip]
RING_SUM = [(dz, flip) for dz, flip in RING if not (CORES_IN_PLANE and (flip or not dz))]
NEAR = ()
PASSED = (4, 3, 5, 2, 6, 1, 7)
SPREAD = [(dz, flip) for dz in HOPS for flip in (0, 1) if (not flip and dz) or (flip and (dz in NEAR or not dz))]
PASS = [dz for dz in PASSED if dz not in NEAR]
PLANE = sorted(
    ((x, y, flip) for x in range(SIDE) for y in range(SIDE) for flip in range(1 + CORES_IN_PLANE) if x or y or flip),
    key=lambda o: (-min(o[0], SIDE - o[0]) - min(o[1], SIDE - o[1]), o),
)
STARTS = (0, 40, 72, 96, 112)


def lanes_between(low, high):
    lane = lax.broadcasted_iota(jnp.int32, (8, LANES), 1)
    return jnp.logical_and(lane >= low, lane < high)


def pack(matrix):
    packed = jnp.zeros((8, LANES), F32)
    for block in range(5):
        rows = matrix[8 * block : 8 * block + 8, :]
        shift = STARTS[block] - 8 * block
        if shift:
            rows = pltpu.roll(rows, shift, 1)
        packed = jnp.where(lanes_between(STARTS[block], STARTS[block] + 40 - 8 * block), rows, packed)
    return packed


def unpack(packed):
    blocks = []
    for block in range(5):
        shift = STARTS[block] - 8 * block
        rows = pltpu.roll(packed, LANES - shift, 1) if shift else packed
        blocks.append(jnp.where(lanes_between(8 * block, 40), rows, 0.0))
    upper = jnp.concatenate(blocks, axis=0)
    lower = jnp.transpose(upper)[:VECS, :]
    lower = jnp.concatenate([lower, jnp.zeros((VECS, LANES - VECS), F32)], axis=1)
    row = lax.broadcasted_iota(jnp.int32, (VECS, LANES), 0)
    col = lax.broadcasted_iota(jnp.int32, (VECS, LANES), 1)
    return jnp.where(col // 8 >= row // 8, upper, lower)


def recursion(gram):
    row = lax.broadcasted_iota(jnp.int32, (VECS, LANES), 0)
    col = lax.broadcasted_iota(jnp.int32, (VECS, LANES), 1)

    def column(j):
        return jnp.broadcast_to(gram[:, j : j + 1], (VECS, LANES))

    def spread(value, i):
        return jnp.broadcast_to(value[i : i + 1, :], (8, LANES))

    def tall(tile):
        return jnp.concatenate([tile] * (VECS // 8), axis=0)

    pairs = jnp.sum(jnp.where(col == row + HIST, gram, 0.0), axis=1, keepdims=True)
    inverses = 1.0 / jnp.broadcast_to(pairs, (VECS, LANES))
    inverse = [spread(inverses, i) for i in range(HIST)]
    products = -column(2 * HIST)
    alphas, steps, diffs = [None] * HIST, [None] * HIST, [None] * HIST
    for i in reversed(range(HIST)):
        alphas[i] = inverse[i] * spread(products, i)
        products = products - tall(alphas[i]) * column(HIST + i)
    scale = spread(column(2 * HIST - 1), HIST - 1) / spread(column(2 * HIST - 1), 2 * HIST - 1)
    products = products * tall(scale)
    for i in range(HIST):
        steps[i] = alphas[i] - inverse[i] * spread(products, HIST + i)
        products = products + tall(steps[i]) * column(i)
        diffs[i] = -alphas[i] * scale
    return steps, diffs, -scale


class Net:
    def __init__(self):
        self.sent, self.open, self.local = [], [], []

    def send(self, source, target, send_sem, recv_sem, **peer):
        copy = pltpu.make_async_remote_copy(
            source, target, send_sem, recv_sem, device_id=peer, device_id_type=MESH
        )
        copy.start()
        self.sent.append(copy)
        self.open.append(copy)
        return copy

    def receive(self, *copies):
        for copy in copies:
            copy.wait_recv()
            self.open = [c for c in self.open if c is not copy]

    def drain(self, *copies):
        for copy in copies:
            copy.wait_send()
            self.sent = [c for c in self.sent if c is not copy]

    def finish(self):
        for copy in self.local:
            copy.wait()
        self.receive(*list(self.open))
        self.drain(*list(self.sent))


def kernel(
    step_hbm, diff_hbm, grad_hbm, out_ref, gram_ref,
    step_v, diff_v, grad_v, hi_send, lo_send, hi_recv, lo_recv, wide, square, staged, plane_parts, ring_parts,
    load_sem, grad_sem, hi_ss, hi_rs, lo_ss, lo_rs, plane_ss, plane_rs, ring_ss, ring_rs, dir_ss, dir_rs, pass_ss, pass_rs,
):
    net = Net()
    me = lax.axis_index("slot")
    col = lax.axis_index("param")
    mate = me + 1 - 2 * lax.rem(me, 2)
    chip, core = me // 2, lax.rem(me, 2)
    own_rows = pl.ds(pl.multiple_of(me * PIECE, PIECE), PIECE)

    def across(dx, dy, flip):
        x, y = col // SIDE, lax.rem(col, SIDE)
        peer = {"param": lax.rem(x + dx, SIDE) * SIDE + lax.rem(y + dy, SIDE)}
        return {**peer, "slot": mate} if flip else peer

    def along(dz, flip):
        return lax.rem(chip + dz, CHIPS) * 2 + (1 - core if flip else core)

    def load(dz):
        rows = pl.ds(pl.multiple_of(lax.rem(chip + dz, CHIPS) * 2 * PIECE, 2 * PIECE), 2 * PIECE)
        return [
            pltpu.make_async_copy(source.at[rows], target.at[rows], load_sem.at[i, dz])
            for i, (source, target) in enumerate(((step_hbm, step_v), (diff_hbm, diff_v)))
        ]

    loads = {dz: load(dz) for dz in HOPS}
    net.local = [c for dz in HOPS for c in loads[dz]]
    grad_load = pltpu.make_async_copy(grad_hbm.at[own_rows], grad_v, grad_sem.at[0])
    for dz in HOPS[:LOADS_FIRST]:
        for copy in loads[dz]:
            copy.start()
    barrier = pltpu.get_barrier_semaphore()
    peers = [{"slot": along(*offset)} for offset in RING] + [across(*offset) for offset in PLANE]
    for peer in peers:
        pl.semaphore_signal(barrier, inc=1, device_id=peer, device_id_type=MESH)
    for dz in HOPS[LOADS_FIRST:]:
        for copy in loads[dz]:
            copy.start()
    grad_load.start()
    net.local.append(grad_load)
    pl.semaphore_wait(barrier, len(peers))
    hi_copies = []
    for part in range(HI_PARTS):
        rows = pl.ds(2 * SPAN * part, 2 * SPAN)
        for i, (dz, flip) in enumerate(RING):
            if not part and (not flip or not dz):
                for copy in loads[dz]:
                    copy.wait()
                    net.local = [c for c in net.local if c is not copy]
            dest = along(dz, flip)
            for half, source in ((0, step_v), (SPAN, diff_v)):
                v = source[pl.ds(pl.multiple_of(dest * PIECE + part * SPAN, 8), SPAN), :]
                at = 2 * SPAN * part + half
                hi_send[dest, at : at + SPAN, :] = v.astype(BF16)
            hi_copies.append(
                net.send(hi_send.at[dest, rows], hi_recv.at[me, rows], hi_ss.at[part, i], hi_rs.at[part, i], slot=dest)
            )
        for half, source in ((0, step_v), (SPAN, diff_v)):
            v = source[pl.ds(pl.multiple_of(me * PIECE + part * SPAN, 8), SPAN), :]
            at = 2 * SPAN * part + half
            hi_recv[me, at : at + SPAN, :] = v.astype(BF16)

    for k in range(SLOTS):
        for half, source in ((0, step_v), (TILE, diff_v)):
            for row in range(0, PIECE, TILE):
                v = source[k * PIECE + row : k * PIECE + row + TILE, :]
                lo_send[k, 2 * row + half : 2 * row + half + TILE, :] = (v - v.astype(BF16).astype(F32)).astype(BF16)

    def send_lo(part):
        rows = pl.ds(2 * CUTS[part], 2 * (CUTS[part + 1] - CUTS[part]))
        copies = []
        for i, offset in enumerate(RING):
            dest = along(*offset)
            copies.append(
                net.send(lo_send.at[dest, rows], lo_recv.at[me, rows], lo_ss.at[part, i], lo_rs.at[part, i], slot=dest)
            )
        return copies

    if HI_DRAIN:
        net.drain(*[c for c in hi_copies if any(c is o for o in net.sent)])
    lo_copies = [send_lo(part) for part in range(LO_EARLY)]
    lo_recv[me] = lo_send[me]
    grad_load.wait()
    net.local = []
    wide[2 * HIST * STRIDE : 2 * HIST * STRIDE + PIECE, :] = grad_v[...].astype(BF16).astype(F32)
    for j in range(2 * HIST + 1, VECS):
        wide[j * STRIDE : j * STRIDE + PIECE, :] = jnp.zeros((PIECE, LANES), F32)

    def widen(k, part):
        at = 2 * SPAN * part
        for j, row in ((k, at), (HIST + k, at + SPAN)):
            rows = pl.ds(pl.multiple_of(j * STRIDE + part * SPAN, 8), SPAN)
            wide[rows, :] = hi_recv[k, row : row + SPAN, :].astype(F32)

    products = jnp.zeros((VECS, VECS), F32)
    for part in range(HI_PARTS):
        widen(me, part)
        for i, (dz, flip) in enumerate(RING):
            net.receive(hi_copies[part * len(RING) + i])
            widen(along(CHIPS - dz, flip), part)
        rows = [wide[pl.ds(r, VECS, stride=STRIDE), :].astype(BF16) for r in range(part * SPAN, (part + 1) * SPAN)]
        flat = jnp.concatenate(rows, axis=1)
        products = products + lax.dot_general(flat, flat, (((1,), (1,)), ((), ())), preferred_element_type=F32)
    square[...] = jnp.zeros((VECS, LANES), F32)
    square[:, :VECS] = products
    packed = pack(square[...])

    def exchange(value, number, parts, mine, peers, send_sems, recv_sems):
        staged[number] = value
        parts[mine] = value
        return [
            net.send(staged.at[number], parts.at[mine], send_sems.at[i], recv_sems.at[i], **peer)
            for i, peer in enumerate(peers)
        ]

    def total(parts):
        values = [parts[k] for k in range(parts.shape[0])]
        while len(values) > 1:
            values = [a + b for a, b in zip(values[::2], values[1::2])]
        return values[0]

    plane_mine = col + COLS * core if CORES_IN_PLANE else col
    ring_mine = chip if CORES_IN_PLANE else me
    ring_peers = [{"slot": along(*offset)} for offset in RING_SUM]
    plane_peers = [across(*offset) for offset in PLANE]
    stages = [(ring_parts, ring_mine, ring_peers, ring_ss, ring_rs), (plane_parts, plane_mine, plane_peers, plane_ss, plane_rs)]
    if not RING_FIRST:
        stages.reverse()
    copies = exchange(packed, 0, *stages[0])
    if RING_FIRST:
        lo_copies += [send_lo(part) for part in range(LO_EARLY, PARTS)]
    net.receive(*reversed(copies))
    copies = exchange(total(stages[0][0]), 1, *stages[1])
    if not RING_FIRST:
        lo_copies += [send_lo(part) for part in range(LO_EARLY, PARTS)]
    net.receive(*reversed(copies))
    gram = unpack(total(stages[1][0]) * (1.0 / (ROWS * LANES * COLS)))
    gram_ref[...] = gram[: 2 * HIST + 1, : 2 * HIST + 1]
    steps, diffs, grad_coeff = recursion(gram)

    def piece(slot, part):
        start = pl.multiple_of(slot * PIECE + CUTS[part], 8)
        return out_ref.at[pl.ds(start, CUTS[part + 1] - CUTS[part])]

    dir_copies = {}
    for n in range(PARTS):
        net.receive(*lo_copies[n])
        for low in range(CUTS[n], CUTS[n + 1], 8):
            acc = grad_coeff * grad_v[low : low + 8, :]
            at = low // TILE * 2 * TILE + low % TILE
            up = low // SPAN * 2 * SPAN + low % SPAN
            for k in range(SLOTS):
                s = hi_recv[k, up : up + 8, :].astype(F32) + lo_recv[k, at : at + 8, :].astype(F32)
                y = hi_recv[k, up + SPAN : up + SPAN + 8, :].astype(F32)
                y = y + lo_recv[k, at + TILE : at + TILE + 8, :].astype(F32)
                acc = acc + steps[k] * s + diffs[k] * y
            out_ref[pl.ds(pl.multiple_of(me * PIECE + low, 8), 8), :] = acc
        for i, (dz, flip) in enumerate(SPREAD):
            dir_copies[n, dz, flip] = net.send(
                piece(me, n), piece(me, n), dir_ss.at[n, i], dir_rs.at[n, i], slot=along(dz, flip)
            )
    for n in range(PARTS):
        for dz in PASS:
            net.receive(dir_copies[n, dz, 0])
            source = along(CHIPS - dz, 0)
            net.send(piece(source, n), piece(source, n), pass_ss.at[n, dz], pass_rs.at[n, dz], slot=mate)
    net.finish()


def call(step, diff, grad):
    dma = pltpu.SemaphoreType.DMA
    return pl.pallas_call(
        kernel,
        out_shape=(pltpu.VMEM((ROWS, LANES), F32), pltpu.VMEM((2 * HIST + 1, 2 * HIST + 1), F32)),
        in_specs=[pl.BlockSpec(memory_space=pltpu.HBM)] * 3,
        out_specs=(pl.BlockSpec(memory_space=pltpu.VMEM), pl.BlockSpec(memory_space=pltpu.VMEM)),
        scratch_shapes=[
            pltpu.VMEM((ROWS, LANES), F32),
            pltpu.VMEM((ROWS, LANES), F32),
            pltpu.VMEM((PIECE, LANES), F32),
            pltpu.VMEM((SLOTS, 2 * PIECE, LANES), BF16),
            pltpu.VMEM((SLOTS, 2 * PIECE, LANES), BF16),
            pltpu.VMEM((SLOTS, 2 * PIECE, LANES), BF16),
            pltpu.VMEM((SLOTS, 2 * PIECE, LANES), BF16),
            pltpu.VMEM((VECS * STRIDE, LANES), F32),
            pltpu.VMEM((VECS, LANES), F32),
            pltpu.VMEM((2, 8, LANES), F32),
            pltpu.VMEM((len(PLANE) + 1, 8, LANES), F32),
            pltpu.VMEM((len(RING_SUM) + 1, 8, LANES), F32),
            dma((2, CHIPS)),
            dma((1,)),
            *[dma((HI_PARTS, SLOTS))] * 2,
            *[dma((PARTS, SLOTS))] * 2,
            *[dma((len(PLANE),))] * 2,
            *[dma((len(RING_SUM),))] * 2,
            *[dma((PARTS, len(SPREAD)))] * 2,
            *[dma((PARTS, CHIPS))] * 2,
        ],
        compiler_params=pltpu.CompilerParams(
            collective_id=0, has_side_effects=True, vmem_limit_bytes=VMEM_LIMIT
        ),
        name="lbfgs",
    )(step, diff, grad)


def write(direction_v, gram_v, direction_hbm, gram_hbm, sem):
    copies = [
        pltpu.make_async_copy(direction_v, direction_hbm, sem.at[0]),
        pltpu.make_async_copy(gram_v, gram_hbm, sem.at[1]),
    ]
    for copy in copies:
        copy.start()
    for copy in copies:
        copy.wait()


def store(direction, gram):
    return pl.pallas_call(
        write,
        out_shape=(
            jax.ShapeDtypeStruct(direction.shape, F32),
            jax.ShapeDtypeStruct(gram.shape, F32),
        ),
        in_specs=[pl.BlockSpec(memory_space=pltpu.VMEM)] * 2,
        out_specs=(pl.BlockSpec(memory_space=pl.ANY), pl.BlockSpec(memory_space=pl.ANY)),
        scratch_shapes=[pltpu.SemaphoreType.DMA((2,))],
        compiler_params=pltpu.CompilerParams(vmem_limit_bytes=2**20),
        name="store",
    )(direction, gram)


def shards(step_hist, diff_hist, gradient):
    shape = (ROWS, LANES)
    direction, gram = store(*call(step_hist.reshape(shape), diff_hist.reshape(shape), gradient.reshape(shape)))
    return direction.reshape(ROWS * LANES), gram


def solution(mesh):
    in_specs = (P("slot", "param"), P("slot", "param"), P("param"))
    out_specs = (P("param"), P())
    return jax.shard_map(shards, mesh=mesh, in_specs=in_specs, out_specs=out_specs, check_vma=False)
```

```python
import functools

import jax
import jax.numpy as jnp
from jax import lax
from jax.experimental import pallas as pl
from jax.experimental.pallas import tpu as pltpu
from jax.sharding import PartitionSpec as P

HIST = 16
SLOTS = 16
COLS = 16
ROWS = 1024
PIECE = ROWS // SLOTS
VECS = 40
LANES = 128
STRIDE = PIECE + 8
F32, BF16 = jnp.float32, jnp.bfloat16
MESH = pl.DeviceIdType.MESH
SIDE = 4
CHIPS = SLOTS // 2
MERGED = True
EARLY_DRAIN = True
HI_AHEAD = True
VMEM_LIMIT = 56 * 2**20
HI_DRAIN = True
LOADS_FIRST = 0
RING_FIRST = True
CORES_IN_PLANE = False
TILE = 16
HI_PARTS = 1
SPAN = PIECE // HI_PARTS
CUTS = (0, 16, 64)
LO_EARLY = 1
PARTS = len(CUTS) - 1


def hops(offset, around):
    return min(offset, around - offset)


HOPS = (4, 3, 5, 2, 6, 1, 7, 0)
RING = [(dz, flip) for dz in HOPS for flip in (0, 1) if dz or flip]
RING_SUM = [(dz, flip) for dz, flip in RING if not (CORES_IN_PLANE and (flip or not dz))]
ORDER = (0, 4, 1, 5, 2, 6, 3, 7)
PASS = (4, 3, 5, 2, 6, 1, 7)
PLANE = sorted(
    ((x, y, flip) for x in range(SIDE) for y in range(SIDE) for flip in range(1 + CORES_IN_PLANE) if x or y or flip),
    key=lambda o: (-hops(o[0], SIDE) - hops(o[1], SIDE), o),
)
STARTS = (0, 40, 72, 96, 112)


def lanes_between(low, high):
    lane = lax.broadcasted_iota(jnp.int32, (8, LANES), 1)
    return jnp.logical_and(lane >= low, lane < high)


def pack(matrix):
    packed = jnp.zeros((8, LANES), F32)
    for block in range(5):
        rows = matrix[8 * block : 8 * block + 8, :]
        shift = STARTS[block] - 8 * block
        if shift:
            rows = pltpu.roll(rows, shift, 1)
        packed = jnp.where(lanes_between(STARTS[block], STARTS[block] + 40 - 8 * block), rows, packed)
    return packed


def unpack(packed):
    blocks = []
    for block in range(5):
        shift = STARTS[block] - 8 * block
        rows = pltpu.roll(packed, LANES - shift, 1) if shift else packed
        blocks.append(jnp.where(lanes_between(8 * block, 40), rows, 0.0))
    upper = jnp.concatenate(blocks, axis=0)
    lower = jnp.transpose(upper)[:VECS, :]
    lower = jnp.concatenate([lower, jnp.zeros((VECS, LANES - VECS), F32)], axis=1)
    row = lax.broadcasted_iota(jnp.int32, (VECS, LANES), 0)
    col = lax.broadcasted_iota(jnp.int32, (VECS, LANES), 1)
    return jnp.where(col // 8 >= row // 8, upper, lower)


def recursion(gram):
    row = lax.broadcasted_iota(jnp.int32, (VECS, LANES), 0)
    col = lax.broadcasted_iota(jnp.int32, (VECS, LANES), 1)

    def column(j):
        return jnp.broadcast_to(gram[:, j : j + 1], (VECS, LANES))

    def spread(value, i):
        return jnp.broadcast_to(value[i : i + 1, :], (8, LANES))

    def tall(tile):
        return jnp.concatenate([tile] * (VECS // 8), axis=0)

    pairs = jnp.sum(jnp.where(col == row + HIST, gram, 0.0), axis=1, keepdims=True)
    inverses = 1.0 / jnp.broadcast_to(pairs, (VECS, LANES))
    inverse = [spread(inverses, i) for i in range(HIST)]
    products = -column(2 * HIST)
    alphas, steps, diffs = [None] * HIST, [None] * HIST, [None] * HIST
    for i in reversed(range(HIST)):
        alphas[i] = inverse[i] * spread(products, i)
        products = products - tall(alphas[i]) * column(HIST + i)
    scale = spread(column(2 * HIST - 1), HIST - 1) / spread(column(2 * HIST - 1), 2 * HIST - 1)
    products = products * tall(scale)
    for i in range(HIST):
        steps[i] = alphas[i] - inverse[i] * spread(products, HIST + i)
        products = products + tall(steps[i]) * column(i)
        diffs[i] = -alphas[i] * scale
    return steps, diffs, -scale


class Net:
    def __init__(self):
        self.sent, self.open, self.local = [], [], []

    def send(self, source, target, send_sem, recv_sem, **peer):
        copy = pltpu.make_async_remote_copy(
            source, target, send_sem, recv_sem, device_id=peer, device_id_type=MESH
        )
        copy.start()
        self.sent.append(copy)
        self.open.append(copy)
        return copy

    def receive(self, *copies):
        for copy in copies:
            copy.wait_recv()
            self.open = [c for c in self.open if c is not copy]

    def drain(self, *copies):
        for copy in copies:
            copy.wait_send()
            self.sent = [c for c in self.sent if c is not copy]

    def finish(self):
        for copy in self.local:
            copy.wait()
        self.receive(*list(self.open))
        self.drain(*list(self.sent))


def kernel(
    step_hbm, diff_hbm, grad_hbm, out_ref, gram_ref,
    step_v, diff_v, grad_v, hi_send, lo_send, hi_recv, lo_recv, wide, square, staged, plane_parts, ring_parts,
    load_sem, grad_sem, hi_ss, hi_rs, lo_ss, lo_rs, plane_ss, plane_rs, ring_ss, ring_rs, dir_ss, dir_rs, pass_ss, pass_rs,
):
    net = Net()
    me = lax.axis_index("slot")
    col = lax.axis_index("param")
    mate = me + 1 - 2 * lax.rem(me, 2)
    chip, core = me // 2, lax.rem(me, 2)
    own_rows = pl.ds(pl.multiple_of(me * PIECE, PIECE), PIECE)

    def across(dx, dy, flip):
        x, y = col // SIDE, lax.rem(col, SIDE)
        peer = {"param": lax.rem(x + dx, SIDE) * SIDE + lax.rem(y + dy, SIDE)}
        return {**peer, "slot": mate} if flip else peer

    def along(dz, flip):
        return lax.rem(chip + dz, CHIPS) * 2 + (1 - core if flip else core)

    def load(dz):
        rows = pl.ds(pl.multiple_of(lax.rem(chip + dz, CHIPS) * 2 * PIECE, 2 * PIECE), 2 * PIECE)
        return [
            pltpu.make_async_copy(source.at[rows], target.at[rows], load_sem.at[i, dz])
            for i, (source, target) in enumerate(((step_hbm, step_v), (diff_hbm, diff_v)))
        ]

    loads = {dz: load(dz) for dz in HOPS}
    net.local = [c for dz in HOPS for c in loads[dz]]
    grad_load = pltpu.make_async_copy(grad_hbm.at[own_rows], grad_v, grad_sem.at[0])
    for dz in HOPS[:LOADS_FIRST]:
        for copy in loads[dz]:
            copy.start()
    barrier = pltpu.get_barrier_semaphore()
    peers = [(hops(dz, CHIPS), {"slot": along(dz, flip)}) for dz, flip in RING]
    peers += [(hops(dx, SIDE) + hops(dy, SIDE), across(dx, dy, flip)) for dx, dy, flip in PLANE]
    peers = [peer for _, peer in sorted(peers, key=lambda p: -p[0])] if MERGED else [peer for _, peer in peers]
    for peer in peers:
        pl.semaphore_signal(barrier, inc=1, device_id=peer, device_id_type=MESH)
    for dz in HOPS[LOADS_FIRST:]:
        for copy in loads[dz]:
            copy.start()
    grad_load.start()
    net.local.append(grad_load)
    pl.semaphore_wait(barrier, len(peers))
    hi_copies = []
    for part in range(HI_PARTS):
        rows = pl.ds(2 * SPAN * part, 2 * SPAN)
        for i, (dz, flip) in enumerate(RING):
            if not part and (not flip or not dz):
                for copy in loads[dz]:
                    copy.wait()
                    net.local = [c for c in net.local if c is not copy]
            dest = along(dz, flip)
            for half, source in ((0, step_v), (SPAN, diff_v)):
                v = source[pl.ds(pl.multiple_of(dest * PIECE + part * SPAN, 8), SPAN), :]
                at = 2 * SPAN * part + half
                hi_send[dest, at : at + SPAN, :] = v.astype(BF16)
            hi_copies.append(
                net.send(hi_send.at[dest, rows], hi_recv.at[me, rows], hi_ss.at[part, i], hi_rs.at[part, i], slot=dest)
            )
        for half, source in ((0, step_v), (SPAN, diff_v)):
            v = source[pl.ds(pl.multiple_of(me * PIECE + part * SPAN, 8), SPAN), :]
            at = 2 * SPAN * part + half
            hi_recv[me, at : at + SPAN, :] = v.astype(BF16)

    for k in range(SLOTS):
        for half, source in ((0, step_v), (TILE, diff_v)):
            for row in range(0, PIECE, TILE):
                v = source[k * PIECE + row : k * PIECE + row + TILE, :]
                lo_send[k, 2 * row + half : 2 * row + half + TILE, :] = (v - v.astype(BF16).astype(F32)).astype(BF16)

    def send_lo(part):
        rows = pl.ds(2 * CUTS[part], 2 * (CUTS[part + 1] - CUTS[part]))
        copies = []
        for i, offset in enumerate(RING):
            dest = along(*offset)
            copies.append(
                net.send(lo_send.at[dest, rows], lo_recv.at[me, rows], lo_ss.at[part, i], lo_rs.at[part, i], slot=dest)
            )
        return copies

    if HI_DRAIN:
        net.drain(*[c for c in hi_copies if any(c is o for o in net.sent)])
    lo_copies = [send_lo(part) for part in range(LO_EARLY)]
    lo_recv[me] = lo_send[me]
    grad_load.wait()
    net.local = []
    wide[2 * HIST * STRIDE : 2 * HIST * STRIDE + PIECE, :] = grad_v[...].astype(BF16).astype(F32)
    for j in range(2 * HIST + 1, VECS):
        wide[j * STRIDE : j * STRIDE + PIECE, :] = jnp.zeros((PIECE, LANES), F32)

    def widen(k, part):
        at = 2 * SPAN * part
        for j, row in ((k, at), (HIST + k, at + SPAN)):
            rows = pl.ds(pl.multiple_of(j * STRIDE + part * SPAN, 8), SPAN)
            wide[rows, :] = hi_recv[k, row : row + SPAN, :].astype(F32)

    products = jnp.zeros((VECS, VECS), F32)
    for part in range(HI_PARTS):
        widen(me, part)
        for i, (dz, flip) in enumerate(RING):
            net.receive(hi_copies[part * len(RING) + i])
            widen(along(CHIPS - dz, flip), part)
        rows = [wide[pl.ds(r, VECS, stride=STRIDE), :].astype(BF16) for r in range(part * SPAN, (part + 1) * SPAN)]
        flat = jnp.concatenate(rows, axis=1)
        products = products + lax.dot_general(flat, flat, (((1,), (1,)), ((), ())), preferred_element_type=F32)
    square[...] = jnp.zeros((VECS, LANES), F32)
    square[:, :VECS] = products
    packed = pack(square[...])

    def exchange(value, number, parts, mine, peers, send_sems, recv_sems):
        staged[number] = value
        parts[mine] = value
        return [
            net.send(staged.at[number], parts.at[mine], send_sems.at[i], recv_sems.at[i], **peer)
            for i, peer in enumerate(peers)
        ]

    def total(parts):
        values = [parts[k] for k in range(parts.shape[0])]
        while len(values) > 1:
            values = [a + b for a, b in zip(values[::2], values[1::2])]
        return values[0]

    plane_mine = col + COLS * core if CORES_IN_PLANE else col
    ring_mine = chip if CORES_IN_PLANE else me
    ring_peers = [{"slot": along(*offset)} for offset in RING_SUM]
    plane_peers = [across(*offset) for offset in PLANE]
    stages = [(ring_parts, ring_mine, ring_peers, ring_ss, ring_rs), (plane_parts, plane_mine, plane_peers, plane_ss, plane_rs)]
    if not RING_FIRST:
        stages.reverse()
    copies = exchange(packed, 0, *stages[0])
    if RING_FIRST:
        lo_copies += [send_lo(part) for part in range(LO_EARLY, PARTS)]
    net.receive(*reversed(copies))
    first = copies
    copies = exchange(total(stages[0][0]), 1, *stages[1])
    if EARLY_DRAIN:
        net.drain(*first)
    if not RING_FIRST:
        lo_copies += [send_lo(part) for part in range(LO_EARLY, PARTS)]
    net.receive(*reversed(copies))
    gram = unpack(total(stages[1][0]) * (1.0 / (ROWS * LANES * COLS)))
    gram_ref[...] = gram[: 2 * HIST + 1, : 2 * HIST + 1]
    steps, diffs, grad_coeff = recursion(gram)

    def piece(slot, part):
        start = pl.multiple_of(slot * PIECE + CUTS[part], 8)
        return out_ref.at[pl.ds(start, CUTS[part + 1] - CUTS[part])]

    def combine(row, at, coeffs, source, span, acc):
        for k in range(SLOTS):
            acc = acc + coeffs[0][k] * source[k, at : at + 8, :].astype(F32)
            acc = acc + coeffs[1][k] * source[k, at + span : at + span + 8, :].astype(F32)
        return acc

    def each(k, n, step):
        copy = pltpu.make_async_remote_copy(
            piece(me, n), piece(me, n), dir_ss.at[n, k], dir_rs.at[n, chip],
            device_id={"slot": 2 * k + core}, device_id_type=MESH,
        )
        pl.when(chip != k)(getattr(copy, step))

    sums = {}
    for low in range(0, PIECE if HI_AHEAD else 0, 8):
        at = low // SPAN * 2 * SPAN + low % SPAN
        sums[low] = combine(low, at, (steps, diffs), hi_recv, SPAN, grad_coeff * grad_v[low : low + 8, :])
    for n in range(PARTS):
        net.receive(*lo_copies[n])
        for low in range(CUTS[n], CUTS[n + 1], 8):
            at = low // TILE * 2 * TILE + low % TILE
            acc = combine(low, at, (steps, diffs), lo_recv, TILE, sums[low])
            out_ref[pl.ds(pl.multiple_of(me * PIECE + low, 8), 8), :] = acc
        for k in ORDER:
            each(k, n, "start")
        net.send(piece(me, n), piece(me, n), pass_ss.at[n, chip], pass_rs.at[n, chip], slot=mate)
    net.drain(*copies, *[c for part_copies in lo_copies for c in part_copies])
    for n in range(PARTS):
        for dz in PASS:
            k = lax.rem(chip + CHIPS - dz, CHIPS)
            source = 2 * k + core
            pltpu.make_async_remote_copy(
                piece(source, n), piece(source, n), dir_ss.at[n, k], dir_rs.at[n, k],
                device_id={"slot": source}, device_id_type=MESH,
            ).wait_recv()
            net.send(piece(source, n), piece(source, n), pass_ss.at[n, k], pass_rs.at[n, k], slot=mate)
    for n in range(PARTS):
        for k in ORDER:
            each(k, n, "wait_send")
    for n in range(PARTS):
        for dz in (0, *PASS):
            k = lax.rem(chip + CHIPS - dz, CHIPS)
            other = 2 * k + 1 - core
            pltpu.make_async_remote_copy(
                piece(other, n), piece(other, n), pass_ss.at[n, k], pass_rs.at[n, k],
                device_id={"slot": mate}, device_id_type=MESH,
            ).wait_recv()
    net.open = []
    net.finish()


def call(step, diff, grad):
    dma = pltpu.SemaphoreType.DMA
    return pl.pallas_call(
        kernel,
        out_shape=(pltpu.VMEM((ROWS, LANES), F32), pltpu.VMEM((2 * HIST + 1, 2 * HIST + 1), F32)),
        in_specs=[pl.BlockSpec(memory_space=pltpu.HBM)] * 3,
        out_specs=(pl.BlockSpec(memory_space=pltpu.VMEM), pl.BlockSpec(memory_space=pltpu.VMEM)),
        scratch_shapes=[
            pltpu.VMEM((ROWS, LANES), F32),
            pltpu.VMEM((ROWS, LANES), F32),
            pltpu.VMEM((PIECE, LANES), F32),
            pltpu.VMEM((SLOTS, 2 * PIECE, LANES), BF16),
            pltpu.VMEM((SLOTS, 2 * PIECE, LANES), BF16),
            pltpu.VMEM((SLOTS, 2 * PIECE, LANES), BF16),
            pltpu.VMEM((SLOTS, 2 * PIECE, LANES), BF16),
            pltpu.VMEM((VECS * STRIDE, LANES), F32),
            pltpu.VMEM((VECS, LANES), F32),
            pltpu.VMEM((2, 8, LANES), F32),
            pltpu.VMEM((len(PLANE) + 1, 8, LANES), F32),
            pltpu.VMEM((len(RING_SUM) + 1, 8, LANES), F32),
            dma((2, CHIPS)),
            dma((1,)),
            *[dma((HI_PARTS, SLOTS))] * 2,
            *[dma((PARTS, SLOTS))] * 2,
            *[dma((len(PLANE),))] * 2,
            *[dma((len(RING_SUM),))] * 2,
            *[dma((PARTS, CHIPS))] * 4,
        ],
        compiler_params=pltpu.CompilerParams(
            collective_id=0, has_side_effects=True, vmem_limit_bytes=VMEM_LIMIT
        ),
        name="lbfgs",
    )(step, diff, grad)


def write(direction_v, gram_v, direction_hbm, gram_hbm, sem):
    copies = [
        pltpu.make_async_copy(direction_v, direction_hbm, sem.at[0]),
        pltpu.make_async_copy(gram_v, gram_hbm, sem.at[1]),
    ]
    for copy in copies:
        copy.start()
    for copy in copies:
        copy.wait()


def store(direction, gram):
    return pl.pallas_call(
        write,
        out_shape=(
            jax.ShapeDtypeStruct(direction.shape, F32),
            jax.ShapeDtypeStruct(gram.shape, F32),
        ),
        in_specs=[pl.BlockSpec(memory_space=pltpu.VMEM)] * 2,
        out_specs=(pl.BlockSpec(memory_space=pl.ANY), pl.BlockSpec(memory_space=pl.ANY)),
        scratch_shapes=[pltpu.SemaphoreType.DMA((2,))],
        compiler_params=pltpu.CompilerParams(vmem_limit_bytes=2**20),
        name="store",
    )(direction, gram)


def shards(step_hist, diff_hist, gradient):
    shape = (ROWS, LANES)
    direction, gram = store(*call(step_hist.reshape(shape), diff_hist.reshape(shape), gradient.reshape(shape)))
    return direction.reshape(ROWS * LANES), gram


def solution(mesh):
    in_specs = (P("slot", "param"), P("slot", "param"), P("param"))
    out_specs = (P("param"), P())
    return jax.shard_map(shards, mesh=mesh, in_specs=in_specs, out_specs=out_specs, check_vma=False)
```

```python
import functools

import jax
import jax.numpy as jnp
from jax import lax
from jax.experimental import pallas as pl
from jax.experimental.pallas import tpu as pltpu
from jax.sharding import PartitionSpec as P

HIST = 16
SLOTS = 16
COLS = 16
ROWS = 1024
PIECE = ROWS // SLOTS
VECS = 40
LANES = 128
STRIDE = PIECE + 8
F32, BF16 = jnp.float32, jnp.bfloat16
MESH = pl.DeviceIdType.MESH
SIDE = 4
CHIPS = SLOTS // 2
STORES = 1
VMEM_LIMIT = 56 * 2**20
LOADS_FIRST = 0
RING_FIRST = True
CORES_IN_PLANE = False
TILE = 16
HI_PARTS = 1
SPAN = PIECE // HI_PARTS
CUTS = (0, 16, 64)
LO_CUTS = (0, 32, 128)
LO_EARLY = 1
PARTS = len(CUTS) - 1
LO_PARTS = len(LO_CUTS) - 1


def hops(offset, around):
    return min(offset, around - offset)


HOPS = (4, 3, 5, 2, 6, 1, 7, 0)
RING = [(dz, flip) for dz in HOPS for flip in (0, 1) if dz or flip]
RING_SUM = [(dz, flip) for dz, flip in RING if not (CORES_IN_PLANE and (flip or not dz))]
ORDER = (0, 4, 1, 5, 2, 6, 3, 7)
PASS = (4, 3, 5, 2, 6, 1, 7)
PLANE = sorted(
    ((x, y, flip) for x in range(SIDE) for y in range(SIDE) for flip in range(1 + CORES_IN_PLANE) if x or y or flip),
    key=lambda o: (-hops(o[0], SIDE) - hops(o[1], SIDE), o),
)
STARTS = (0, 40, 72, 96, 112)


def lanes_between(low, high):
    lane = lax.broadcasted_iota(jnp.int32, (8, LANES), 1)
    return jnp.logical_and(lane >= low, lane < high)


def pack(matrix):
    packed = jnp.zeros((8, LANES), F32)
    for block in range(5):
        rows = matrix[8 * block : 8 * block + 8, :]
        shift = STARTS[block] - 8 * block
        if shift:
            rows = pltpu.roll(rows, shift, 1)
        packed = jnp.where(lanes_between(STARTS[block], STARTS[block] + 40 - 8 * block), rows, packed)
    return packed


def unpack(packed):
    blocks = []
    for block in range(5):
        shift = STARTS[block] - 8 * block
        rows = pltpu.roll(packed, LANES - shift, 1) if shift else packed
        blocks.append(jnp.where(lanes_between(8 * block, 40), rows, 0.0))
    upper = jnp.concatenate(blocks, axis=0)
    lower = jnp.transpose(upper)[:VECS, :]
    lower = jnp.concatenate([lower, jnp.zeros((VECS, LANES - VECS), F32)], axis=1)
    row = lax.broadcasted_iota(jnp.int32, (VECS, LANES), 0)
    col = lax.broadcasted_iota(jnp.int32, (VECS, LANES), 1)
    return jnp.where(col // 8 >= row // 8, upper, lower)


def recursion(gram):
    row = lax.broadcasted_iota(jnp.int32, (VECS, LANES), 0)
    col = lax.broadcasted_iota(jnp.int32, (VECS, LANES), 1)

    def column(j):
        return jnp.broadcast_to(gram[:, j : j + 1], (VECS, LANES))

    def spread(value, i):
        return jnp.broadcast_to(value[i : i + 1, :], (8, LANES))

    def tall(tile):
        return jnp.concatenate([tile] * (VECS // 8), axis=0)

    pairs = jnp.sum(jnp.where(col == row + HIST, gram, 0.0), axis=1, keepdims=True)
    inverses = 1.0 / jnp.broadcast_to(pairs, (VECS, LANES))
    inverse = [spread(inverses, i) for i in range(HIST)]
    products = -column(2 * HIST)
    alphas, steps, diffs = [None] * HIST, [None] * HIST, [None] * HIST
    for i in reversed(range(HIST)):
        alphas[i] = inverse[i] * spread(products, i)
        products = products - tall(alphas[i]) * column(HIST + i)
    scale = spread(column(2 * HIST - 1), HIST - 1) / spread(column(2 * HIST - 1), 2 * HIST - 1)
    products = products * tall(scale)
    for i in range(HIST):
        steps[i] = alphas[i] - inverse[i] * spread(products, HIST + i)
        products = products + tall(steps[i]) * column(i)
        diffs[i] = -alphas[i] * scale
    return steps, diffs, -scale


class Net:
    def __init__(self):
        self.sent, self.open, self.local = [], [], []

    def send(self, source, target, send_sem, recv_sem, **peer):
        copy = pltpu.make_async_remote_copy(
            source, target, send_sem, recv_sem, device_id=peer, device_id_type=MESH
        )
        copy.start()
        self.sent.append(copy)
        self.open.append(copy)
        return copy

    def receive(self, *copies):
        for copy in copies:
            copy.wait_recv()
            self.open = [c for c in self.open if c is not copy]

    def drain(self, *copies):
        for copy in copies:
            copy.wait_send()
            self.sent = [c for c in self.sent if c is not copy]

    def finish(self):
        for copy in self.local:
            copy.wait()
        self.receive(*list(self.open))
        self.drain(*list(self.sent))


def kernel(
    step_hbm, diff_hbm, grad_hbm, out_ref, gram_ref,
    step_v, diff_v, grad_v, hi_send, lo_send, hi_recv, lo_recv, wide, square, staged, plane_parts, ring_parts,
    load_sem, grad_sem, hi_ss, hi_rs, lo_ss, lo_rs, plane_ss, plane_rs, ring_ss, ring_rs, dir_ss, dir_rs, pass_ss, pass_rs,
):
    net = Net()
    me = lax.axis_index("slot")
    col = lax.axis_index("param")
    mate = me + 1 - 2 * lax.rem(me, 2)
    chip, core = me // 2, lax.rem(me, 2)
    own_rows = pl.ds(pl.multiple_of(me * PIECE, PIECE), PIECE)

    def across(dx, dy, flip):
        x, y = col // SIDE, lax.rem(col, SIDE)
        peer = {"param": lax.rem(x + dx, SIDE) * SIDE + lax.rem(y + dy, SIDE)}
        return {**peer, "slot": mate} if flip else peer

    def along(dz, flip):
        return lax.rem(chip + dz, CHIPS) * 2 + (1 - core if flip else core)

    def load(dz):
        rows = pl.ds(pl.multiple_of(lax.rem(chip + dz, CHIPS) * 2 * PIECE, 2 * PIECE), 2 * PIECE)
        return [
            pltpu.make_async_copy(source.at[rows], target.at[rows], load_sem.at[i, dz])
            for i, (source, target) in enumerate(((step_hbm, step_v), (diff_hbm, diff_v)))
        ]

    loads = {dz: load(dz) for dz in HOPS}
    net.local = [c for dz in HOPS for c in loads[dz]]
    grad_load = pltpu.make_async_copy(grad_hbm.at[own_rows], grad_v, grad_sem.at[0])
    for dz in HOPS[:LOADS_FIRST]:
        for copy in loads[dz]:
            copy.start()
    barrier = pltpu.get_barrier_semaphore()
    peers = [{"slot": along(dz, flip)} for dz, flip in RING]
    peers += [across(dx, dy, flip) for dx, dy, flip in PLANE]
    for peer in peers:
        pl.semaphore_signal(barrier, inc=1, device_id=peer, device_id_type=MESH)
    for dz in HOPS[LOADS_FIRST:]:
        for copy in loads[dz]:
            copy.start()
    grad_load.start()
    net.local.append(grad_load)
    pl.semaphore_wait(barrier, len(peers))
    hi_copies = []
    for part in range(HI_PARTS):
        rows = pl.ds(2 * SPAN * part, 2 * SPAN)
        for i, (dz, flip) in enumerate(RING):
            if not part and (not flip or not dz):
                for copy in loads[dz]:
                    copy.wait()
                    net.local = [c for c in net.local if c is not copy]
            dest = along(dz, flip)
            for half, source in ((0, step_v), (SPAN, diff_v)):
                v = source[pl.ds(pl.multiple_of(dest * PIECE + part * SPAN, 8), SPAN), :]
                at = 2 * SPAN * part + half
                hi_send[dest, at : at + SPAN, :] = v.astype(BF16)
            hi_copies.append(
                net.send(hi_send.at[dest, rows], hi_recv.at[me, rows], hi_ss.at[part, i], hi_rs.at[part, i], slot=dest)
            )
        for half, source in ((0, step_v), (SPAN, diff_v)):
            v = source[pl.ds(pl.multiple_of(me * PIECE + part * SPAN, 8), SPAN), :]
            at = 2 * SPAN * part + half
            hi_recv[me, at : at + SPAN, :] = v.astype(BF16)

    for k in range(SLOTS):
        for half, source in ((0, step_v), (TILE, diff_v)):
            for row in range(0, PIECE, TILE):
                v = source[k * PIECE + row : k * PIECE + row + TILE, :]
                lo_send[k, 2 * row + half : 2 * row + half + TILE, :] = (v - v.astype(BF16).astype(F32)).astype(BF16)

    def together(ref, send_sem, recv_sem):
        return pltpu.make_async_remote_copy(
            ref, ref, send_sem, recv_sem, device_id={"slot": mate}, device_id_type=MESH
        )

    def send_lo(part):
        rows = pl.ds(LO_CUTS[part], LO_CUTS[part + 1] - LO_CUTS[part])
        for offset in RING:
            dest = along(*offset)
            pltpu.make_async_remote_copy(
                lo_send.at[dest, rows], lo_recv.at[me, rows], lo_ss.at[part], lo_rs.at[part],
                device_id={"slot": dest}, device_id_type=MESH,
            ).start()
        return together(lo_recv.at[pl.ds(0, len(RING)), rows], lo_ss.at[part], lo_rs.at[part])

    net.drain(*hi_copies)
    lo_copies = [send_lo(part) for part in range(LO_EARLY)]
    lo_recv[me] = lo_send[me]
    grad_load.wait()
    net.local = []
    wide[2 * HIST * STRIDE : 2 * HIST * STRIDE + PIECE, :] = grad_v[...].astype(BF16).astype(F32)
    for j in range(2 * HIST + 1, VECS):
        wide[j * STRIDE : j * STRIDE + PIECE, :] = jnp.zeros((PIECE, LANES), F32)

    def widen(k, part):
        at = 2 * SPAN * part
        for j, row in ((k, at), (HIST + k, at + SPAN)):
            rows = pl.ds(pl.multiple_of(j * STRIDE + part * SPAN, 8), SPAN)
            wide[rows, :] = hi_recv[k, row : row + SPAN, :].astype(F32)

    products = jnp.zeros((VECS, VECS), F32)
    for part in range(HI_PARTS):
        widen(me, part)
        for i, (dz, flip) in enumerate(RING):
            net.receive(hi_copies[part * len(RING) + i])
            widen(along(CHIPS - dz, flip), part)
        rows = [wide[pl.ds(r, VECS, stride=STRIDE), :].astype(BF16) for r in range(part * SPAN, (part + 1) * SPAN)]
        flat = jnp.concatenate(rows, axis=1)
        products = products + lax.dot_general(flat, flat, (((1,), (1,)), ((), ())), preferred_element_type=F32)
    square[...] = jnp.zeros((VECS, LANES), F32)
    square[:, :VECS] = products
    packed = pack(square[...])

    def exchange(value, number, parts, mine, peers, send_sems, recv_sems):
        staged[number] = value
        parts[mine] = value
        return [
            net.send(staged.at[number], parts.at[mine], send_sems.at[i], recv_sems.at[i], **peer)
            for i, peer in enumerate(peers)
        ]

    def total(parts):
        values = [parts[k] for k in range(parts.shape[0])]
        while len(values) > 1:
            values = [a + b for a, b in zip(values[::2], values[1::2])]
        return values[0]

    plane_mine = col + COLS * core if CORES_IN_PLANE else col
    ring_mine = chip if CORES_IN_PLANE else me
    ring_peers = [{"slot": along(*offset)} for offset in RING_SUM]
    plane_peers = [across(*offset) for offset in PLANE]
    stages = [(ring_parts, ring_mine, ring_peers, ring_ss, ring_rs), (plane_parts, plane_mine, plane_peers, plane_ss, plane_rs)]
    if not RING_FIRST:
        stages.reverse()
    copies = exchange(packed, 0, *stages[0])
    if RING_FIRST:
        lo_copies += [send_lo(part) for part in range(LO_EARLY, LO_PARTS)]
    net.receive(*reversed(copies))
    first = copies
    copies = exchange(total(stages[0][0]), 1, *stages[1])
    net.drain(*first)
    if not RING_FIRST:
        lo_copies += [send_lo(part) for part in range(LO_EARLY, LO_PARTS)]
    net.receive(*reversed(copies))
    gram = unpack(total(stages[1][0]) * (1.0 / (ROWS * LANES * COLS)))
    gram_ref[...] = gram[: 2 * HIST + 1, : 2 * HIST + 1]
    steps, diffs, grad_coeff = recursion(gram)

    def piece(slot, part):
        start = pl.multiple_of(slot * PIECE + CUTS[part], 8)
        return out_ref.at[pl.ds(start, CUTS[part + 1] - CUTS[part])]

    def combine(row, at, coeffs, source, span, acc):
        for k in range(SLOTS):
            acc = acc + coeffs[0][k] * source[k, at : at + 8, :].astype(F32)
            acc = acc + coeffs[1][k] * source[k, at + span : at + span + 8, :].astype(F32)
        return acc

    def send_piece(k, n):
        copy = pltpu.make_async_remote_copy(
            piece(me, n), piece(me, n), dir_ss.at[n], dir_rs.at[n, chip],
            device_id={"slot": 2 * k + core}, device_id_type=MESH,
        )
        pl.when(chip != k)(copy.start)

    def pass_on(source, n):
        pltpu.make_async_remote_copy(
            piece(source, n), piece(source, n), pass_ss.at[n], pass_rs.at[n],
            device_id={"slot": mate}, device_id_type=MESH,
        ).start()

    def pieces(number, n):
        return out_ref.at[pl.ds(0, number * (CUTS[n + 1] - CUTS[n]))]

    sums = {}
    for low in range(0, PIECE, 8):
        at = low // SPAN * 2 * SPAN + low % SPAN
        sums[low] = combine(low, at, (steps, diffs), hi_recv, SPAN, grad_coeff * grad_v[low : low + 8, :])
    for n in range(PARTS):
        arrived = sum(low < 2 * CUTS[n] for low in LO_CUTS[:-1]) if n else 0
        needed = sum(low < 2 * CUTS[n + 1] for low in LO_CUTS[:-1])
        for part in range(arrived, needed):
            lo_copies[part].wait_recv()
        for low in range(CUTS[n], CUTS[n + 1], 8):
            at = low // TILE * 2 * TILE + low % TILE
            acc = combine(low, at, (steps, diffs), lo_recv, TILE, sums[low])
            out_ref[pl.ds(pl.multiple_of(me * PIECE + low, 8), 8), :] = acc
        for k in ORDER:
            send_piece(k, n)
        pass_on(me, n)
    net.drain(*copies)
    for copy in lo_copies:
        copy.wait_send()
    for n in range(PARTS):
        for dz in PASS:
            k = lax.rem(chip + CHIPS - dz, CHIPS)
            source = 2 * k + core
            together(piece(source, n), dir_ss.at[n], dir_rs.at[n, k]).wait_recv()
            pass_on(source, n)
    net.finish()
    for n in range(PARTS):
        together(pieces(CHIPS - 1, n), dir_ss.at[n], pass_rs.at[n]).wait_send()
        together(pieces(CHIPS, n), pass_ss.at[n], pass_rs.at[n]).wait_send()
    for n in range(PARTS):
        together(pieces(CHIPS, n), pass_ss.at[n], pass_rs.at[n]).wait_recv()


def call(step, diff, grad):
    dma = pltpu.SemaphoreType.DMA
    return pl.pallas_call(
        kernel,
        out_shape=(pltpu.VMEM((ROWS, LANES), F32), pltpu.VMEM((2 * HIST + 1, 2 * HIST + 1), F32)),
        in_specs=[pl.BlockSpec(memory_space=pltpu.HBM)] * 3,
        out_specs=(pl.BlockSpec(memory_space=pltpu.VMEM), pl.BlockSpec(memory_space=pltpu.VMEM)),
        scratch_shapes=[
            pltpu.VMEM((ROWS, LANES), F32),
            pltpu.VMEM((ROWS, LANES), F32),
            pltpu.VMEM((PIECE, LANES), F32),
            pltpu.VMEM((SLOTS, 2 * PIECE, LANES), BF16),
            pltpu.VMEM((SLOTS, 2 * PIECE, LANES), BF16),
            pltpu.VMEM((SLOTS, 2 * PIECE, LANES), BF16),
            pltpu.VMEM((SLOTS, 2 * PIECE, LANES), BF16),
            pltpu.VMEM((VECS * STRIDE, LANES), F32),
            pltpu.VMEM((VECS, LANES), F32),
            pltpu.VMEM((2, 8, LANES), F32),
            pltpu.VMEM((len(PLANE) + 1, 8, LANES), F32),
            pltpu.VMEM((len(RING_SUM) + 1, 8, LANES), F32),
            dma((2, CHIPS)),
            dma((1,)),
            *[dma((HI_PARTS, SLOTS))] * 2,
            *[dma((LO_PARTS,))] * 2,
            *[dma((len(PLANE),))] * 2,
            *[dma((len(RING_SUM),))] * 2,
            dma((PARTS,)),
            dma((PARTS, CHIPS)),
            *[dma((PARTS,))] * 2,
        ],
        compiler_params=pltpu.CompilerParams(
            collective_id=0, has_side_effects=True, vmem_limit_bytes=VMEM_LIMIT
        ),
        name="lbfgs",
    )(step, diff, grad)


def write(direction_v, gram_v, direction_hbm, gram_hbm, sem):
    copies = [pltpu.make_async_copy(gram_v, gram_hbm, sem.at[STORES])]
    for i in range(STORES):
        rows = pl.ds(i * ROWS // STORES, ROWS // STORES)
        copies.append(pltpu.make_async_copy(direction_v.at[rows], direction_hbm.at[rows], sem.at[i]))
    for copy in copies:
        copy.start()
    for copy in copies:
        copy.wait()


def store(direction, gram):
    return pl.pallas_call(
        write,
        out_shape=(
            jax.ShapeDtypeStruct(direction.shape, F32),
            jax.ShapeDtypeStruct(gram.shape, F32),
        ),
        in_specs=[pl.BlockSpec(memory_space=pltpu.VMEM)] * 2,
        out_specs=(pl.BlockSpec(memory_space=pl.ANY), pl.BlockSpec(memory_space=pl.ANY)),
        scratch_shapes=[pltpu.SemaphoreType.DMA((STORES + 1,))],
        compiler_params=pltpu.CompilerParams(vmem_limit_bytes=2**20),
        name="store",
    )(direction, gram)


def shards(step_hist, diff_hist, gradient):
    shape = (ROWS, LANES)
    direction, gram = store(*call(step_hist.reshape(shape), diff_hist.reshape(shape), gradient.reshape(shape)))
    return direction.reshape(ROWS * LANES), gram


def solution(mesh):
    in_specs = (P("slot", "param"), P("slot", "param"), P("param"))
    out_specs = (P("param"), P())
    return jax.shard_map(shards, mesh=mesh, in_specs=in_specs, out_specs=out_specs, check_vma=False)
```

```python
import functools

import jax
import jax.numpy as jnp
from jax import lax
from jax.experimental import pallas as pl
from jax.experimental.pallas import tpu as pltpu
from jax.sharding import PartitionSpec as P

HIST = 16
SLOTS = 16
COLS = 16
ROWS = 1024
PIECE = ROWS // SLOTS
VECS = 40
LANES = 128
STRIDE = PIECE + 8
F32, BF16 = jnp.float32, jnp.bfloat16
MESH = pl.DeviceIdType.MESH
SIDE = 4
CHIPS = SLOTS // 2
STORES = 1
VMEM_LIMIT = 56 * 2**20
LOADS_FIRST = 0
RING_FIRST = True
CORES_IN_PLANE = False
TILE = 16
HI_PARTS = 1
SPAN = PIECE // HI_PARTS
CUTS = (0, 16, 64)
LO_CUTS = (0, 32, 128)
LO_EARLY = 1
PARTS = len(CUTS) - 1
LO_PARTS = len(LO_CUTS) - 1


def hops(offset, around):
    return min(offset, around - offset)


HOPS = (4, 3, 5, 2, 6, 1, 7, 0)
RING = [(dz, flip) for dz in HOPS for flip in (0, 1) if dz or flip]
RING_SUM = [(dz, flip) for dz, flip in RING if not (CORES_IN_PLANE and (flip or not dz))]
ORDER = (0, 4, 1, 5, 2, 6, 3, 7)
PASS = (4, 3, 5, 2, 6, 1, 7)
PLANE = sorted(
    ((x, y, flip) for x in range(SIDE) for y in range(SIDE) for flip in range(1 + CORES_IN_PLANE) if x or y or flip),
    key=lambda o: (-hops(o[0], SIDE) - hops(o[1], SIDE), o),
)
STARTS = (0, 40, 72, 96, 112)


def lanes_between(low, high):
    lane = lax.broadcasted_iota(jnp.int32, (8, LANES), 1)
    return jnp.logical_and(lane >= low, lane < high)


def pack(matrix):
    packed = jnp.zeros((8, LANES), F32)
    for block in range(5):
        rows = matrix[8 * block : 8 * block + 8, :]
        shift = STARTS[block] - 8 * block
        if shift:
            rows = pltpu.roll(rows, shift, 1)
        packed = jnp.where(lanes_between(STARTS[block], STARTS[block] + 40 - 8 * block), rows, packed)
    return packed


def unpack(packed):
    blocks = []
    for block in range(5):
        shift = STARTS[block] - 8 * block
        rows = pltpu.roll(packed, LANES - shift, 1) if shift else packed
        blocks.append(jnp.where(lanes_between(8 * block, 40), rows, 0.0))
    upper = jnp.concatenate(blocks, axis=0)
    lower = jnp.transpose(upper)[:VECS, :]
    lower = jnp.concatenate([lower, jnp.zeros((VECS, LANES - VECS), F32)], axis=1)
    row = lax.broadcasted_iota(jnp.int32, (VECS, LANES), 0)
    col = lax.broadcasted_iota(jnp.int32, (VECS, LANES), 1)
    return jnp.where(col // 8 >= row // 8, upper, lower)


def recursion(gram):
    row = lax.broadcasted_iota(jnp.int32, (VECS, LANES), 0)
    col = lax.broadcasted_iota(jnp.int32, (VECS, LANES), 1)

    def column(j):
        return jnp.broadcast_to(gram[:, j : j + 1], (VECS, LANES))

    def spread(value, i):
        return jnp.broadcast_to(value[i : i + 1, :], (8, LANES))

    def tall(tile):
        return jnp.concatenate([tile] * (VECS // 8), axis=0)

    pairs = jnp.sum(jnp.where(col == row + HIST, gram, 0.0), axis=1, keepdims=True)
    inverses = 1.0 / jnp.broadcast_to(pairs, (VECS, LANES))
    inverse = [spread(inverses, i) for i in range(HIST)]
    products = -column(2 * HIST)
    alphas, steps, diffs = [None] * HIST, [None] * HIST, [None] * HIST
    for i in reversed(range(HIST)):
        alphas[i] = inverse[i] * spread(products, i)
        products = products - tall(alphas[i]) * column(HIST + i)
    scale = spread(column(2 * HIST - 1), HIST - 1) / spread(column(2 * HIST - 1), 2 * HIST - 1)
    products = products * tall(scale)
    for i in range(HIST):
        steps[i] = alphas[i] - inverse[i] * spread(products, HIST + i)
        products = products + tall(steps[i]) * column(i)
        diffs[i] = -alphas[i] * scale
    return steps, diffs, -scale


def kernel(
    step_hbm, diff_hbm, grad_hbm, out_ref, gram_ref,
    step_v, diff_v, grad_v, hi_send, lo_send, hi_recv, lo_recv, wide, square, staged, plane_parts, ring_parts,
    load_sem, grad_sem, hi_ss, hi_rs, lo_ss, lo_rs, plane_ss, plane_rs, ring_ss, ring_rs, dir_ss, dir_rs, pass_ss, pass_rs,
):
    me = lax.axis_index("slot")
    col = lax.axis_index("param")
    mate = me + 1 - 2 * lax.rem(me, 2)
    chip, core = me // 2, lax.rem(me, 2)
    own_rows = pl.ds(pl.multiple_of(me * PIECE, PIECE), PIECE)

    def across(dx, dy, flip):
        x, y = col // SIDE, lax.rem(col, SIDE)
        peer = {"param": lax.rem(x + dx, SIDE) * SIDE + lax.rem(y + dy, SIDE)}
        return {**peer, "slot": mate} if flip else peer

    def along(dz, flip):
        return lax.rem(chip + dz, CHIPS) * 2 + (1 - core if flip else core)

    def load(dz):
        rows = pl.ds(pl.multiple_of(lax.rem(chip + dz, CHIPS) * 2 * PIECE, 2 * PIECE), 2 * PIECE)
        return [
            pltpu.make_async_copy(source.at[rows], target.at[rows], load_sem.at[i, dz])
            for i, (source, target) in enumerate(((step_hbm, step_v), (diff_hbm, diff_v)))
        ]

    loads = {dz: load(dz) for dz in HOPS}
    grad_load = pltpu.make_async_copy(grad_hbm.at[own_rows], grad_v, grad_sem.at[0])
    for dz in HOPS[:LOADS_FIRST]:
        for copy in loads[dz]:
            copy.start()
    barrier = pltpu.get_barrier_semaphore()
    peers = [{"slot": along(dz, flip)} for dz, flip in RING]
    peers += [across(dx, dy, flip) for dx, dy, flip in PLANE]
    for peer in peers:
        pl.semaphore_signal(barrier, inc=1, device_id=peer, device_id_type=MESH)
    for dz in HOPS[LOADS_FIRST:]:
        for copy in loads[dz]:
            copy.start()
    grad_load.start()
    pl.semaphore_wait(barrier, len(peers))
    hi_copies = []
    for part in range(HI_PARTS):
        rows = pl.ds(2 * SPAN * part, 2 * SPAN)
        for i, (dz, flip) in enumerate(RING):
            if not part and (not flip or not dz):
                for copy in loads[dz]:
                    copy.wait()
            dest = along(dz, flip)
            for half, source in ((0, step_v), (SPAN, diff_v)):
                v = source[pl.ds(pl.multiple_of(dest * PIECE + part * SPAN, 8), SPAN), :]
                at = 2 * SPAN * part + half
                hi_send[dest, at : at + SPAN, :] = v.astype(BF16)
            copy = pltpu.make_async_remote_copy(
                hi_send.at[dest, rows], hi_recv.at[me, rows], hi_ss.at[part], hi_rs.at[part, i],
                device_id={"slot": dest}, device_id_type=MESH,
            )
            copy.start()
            hi_copies.append(copy)
        for half, source in ((0, step_v), (SPAN, diff_v)):
            v = source[pl.ds(pl.multiple_of(me * PIECE + part * SPAN, 8), SPAN), :]
            at = 2 * SPAN * part + half
            hi_recv[me, at : at + SPAN, :] = v.astype(BF16)

    for k in range(SLOTS):
        for half, source in ((0, step_v), (TILE, diff_v)):
            for row in range(0, PIECE, TILE):
                v = source[k * PIECE + row : k * PIECE + row + TILE, :]
                lo_send[k, 2 * row + half : 2 * row + half + TILE, :] = (v - v.astype(BF16).astype(F32)).astype(BF16)

    def together(ref, send_sem, recv_sem):
        return pltpu.make_async_remote_copy(
            ref, ref, send_sem, recv_sem, device_id={"slot": mate}, device_id_type=MESH
        )

    def send_lo(part):
        rows = pl.ds(LO_CUTS[part], LO_CUTS[part + 1] - LO_CUTS[part])
        for offset in RING:
            dest = along(*offset)
            pltpu.make_async_remote_copy(
                lo_send.at[dest, rows], lo_recv.at[me, rows], lo_ss.at[part], lo_rs.at[part],
                device_id={"slot": dest}, device_id_type=MESH,
            ).start()
        return together(lo_recv.at[pl.ds(0, len(RING)), rows], lo_ss.at[part], lo_rs.at[part])

    for part in range(HI_PARTS):
        rows = pl.ds(2 * SPAN * part, 2 * SPAN)
        together(hi_recv.at[pl.ds(0, len(RING)), rows], hi_ss.at[part], hi_rs.at[part, 0]).wait_send()
    lo_copies = [send_lo(part) for part in range(LO_EARLY)]
    lo_recv[me] = lo_send[me]
    grad_load.wait()
    wide[2 * HIST * STRIDE : 2 * HIST * STRIDE + PIECE, :] = grad_v[...].astype(BF16).astype(F32)
    for j in range(2 * HIST + 1, VECS):
        wide[j * STRIDE : j * STRIDE + PIECE, :] = jnp.zeros((PIECE, LANES), F32)

    def widen(k, part):
        at = 2 * SPAN * part
        for j, row in ((k, at), (HIST + k, at + SPAN)):
            rows = pl.ds(pl.multiple_of(j * STRIDE + part * SPAN, 8), SPAN)
            wide[rows, :] = hi_recv[k, row : row + SPAN, :].astype(F32)

    products = jnp.zeros((VECS, VECS), F32)
    for part in range(HI_PARTS):
        widen(me, part)
        for i, (dz, flip) in enumerate(RING):
            hi_copies[part * len(RING) + i].wait_recv()
            widen(along(CHIPS - dz, flip), part)
        rows = [wide[pl.ds(r, VECS, stride=STRIDE), :].astype(BF16) for r in range(part * SPAN, (part + 1) * SPAN)]
        flat = jnp.concatenate(rows, axis=1)
        products = products + lax.dot_general(flat, flat, (((1,), (1,)), ((), ())), preferred_element_type=F32)
    square[...] = jnp.zeros((VECS, LANES), F32)
    square[:, :VECS] = products
    packed = pack(square[...])

    def exchange(value, number, parts, mine, peers, send_sems, recv_sems):
        staged[number] = value
        parts[mine] = value
        for peer in peers:
            pltpu.make_async_remote_copy(
                staged.at[number], parts.at[mine], send_sems.at[0], recv_sems.at[0],
                device_id=peer, device_id_type=MESH,
            ).start()
        return together(parts.at[pl.ds(0, len(peers))], send_sems.at[0], recv_sems.at[0])

    def total(parts):
        values = [parts[k] for k in range(parts.shape[0])]
        while len(values) > 1:
            values = [a + b for a, b in zip(values[::2], values[1::2])]
        return values[0]

    plane_mine = col + COLS * core if CORES_IN_PLANE else col
    ring_mine = chip if CORES_IN_PLANE else me
    ring_peers = [{"slot": along(*offset)} for offset in RING_SUM]
    plane_peers = [across(*offset) for offset in PLANE]
    stages = [(ring_parts, ring_mine, ring_peers, ring_ss, ring_rs), (plane_parts, plane_mine, plane_peers, plane_ss, plane_rs)]
    if not RING_FIRST:
        stages.reverse()
    copies = exchange(packed, 0, *stages[0])
    if RING_FIRST:
        lo_copies += [send_lo(part) for part in range(LO_EARLY, LO_PARTS)]
    copies.wait_recv()
    first = copies
    copies = exchange(total(stages[0][0]), 1, *stages[1])
    first.wait_send()
    if not RING_FIRST:
        lo_copies += [send_lo(part) for part in range(LO_EARLY, LO_PARTS)]
    copies.wait_recv()
    gram = unpack(total(stages[1][0]) * (1.0 / (ROWS * LANES * COLS)))
    gram_ref[...] = gram[: 2 * HIST + 1, : 2 * HIST + 1]
    steps, diffs, grad_coeff = recursion(gram)

    def piece(slot, part):
        start = pl.multiple_of(slot * PIECE + CUTS[part], 8)
        return out_ref.at[pl.ds(start, CUTS[part + 1] - CUTS[part])]

    def combine(row, at, coeffs, source, span, acc):
        for k in range(SLOTS):
            acc = acc + coeffs[0][k] * source[k, at : at + 8, :].astype(F32)
            acc = acc + coeffs[1][k] * source[k, at + span : at + span + 8, :].astype(F32)
        return acc

    def send_piece(k, n):
        copy = pltpu.make_async_remote_copy(
            piece(me, n), piece(me, n), dir_ss.at[n], dir_rs.at[n, chip],
            device_id={"slot": 2 * k + core}, device_id_type=MESH,
        )
        pl.when(chip != k)(copy.start)

    def pass_on(source, n):
        pltpu.make_async_remote_copy(
            piece(source, n), piece(source, n), pass_ss.at[n], pass_rs.at[n],
            device_id={"slot": mate}, device_id_type=MESH,
        ).start()

    def pieces(number, n):
        return out_ref.at[pl.ds(0, number * (CUTS[n + 1] - CUTS[n]))]

    sums = {}
    for low in range(0, PIECE, 8):
        at = low // SPAN * 2 * SPAN + low % SPAN
        sums[low] = combine(low, at, (steps, diffs), hi_recv, SPAN, grad_coeff * grad_v[low : low + 8, :])
    for n in range(PARTS):
        arrived = sum(low < 2 * CUTS[n] for low in LO_CUTS[:-1]) if n else 0
        needed = sum(low < 2 * CUTS[n + 1] for low in LO_CUTS[:-1])
        for part in range(arrived, needed):
            lo_copies[part].wait_recv()
        for low in range(CUTS[n], CUTS[n + 1], 8):
            at = low // TILE * 2 * TILE + low % TILE
            acc = combine(low, at, (steps, diffs), lo_recv, TILE, sums[low])
            out_ref[pl.ds(pl.multiple_of(me * PIECE + low, 8), 8), :] = acc
        for k in ORDER:
            send_piece(k, n)
        pass_on(me, n)
    copies.wait_send()
    for copy in lo_copies:
        copy.wait_send()
    for n in range(PARTS):
        for dz in PASS:
            k = lax.rem(chip + CHIPS - dz, CHIPS)
            source = 2 * k + core
            together(piece(source, n), dir_ss.at[n], dir_rs.at[n, k]).wait_recv()
            pass_on(source, n)
    for n in range(PARTS):
        together(pieces(CHIPS - 1, n), dir_ss.at[n], pass_rs.at[n]).wait_send()
        together(pieces(CHIPS, n), pass_ss.at[n], pass_rs.at[n]).wait_send()
    for n in range(PARTS):
        together(pieces(CHIPS, n), pass_ss.at[n], pass_rs.at[n]).wait_recv()


def call(step, diff, grad):
    dma = pltpu.SemaphoreType.DMA
    return pl.pallas_call(
        kernel,
        out_shape=(pltpu.VMEM((ROWS, LANES), F32), pltpu.VMEM((2 * HIST + 1, 2 * HIST + 1), F32)),
        in_specs=[pl.BlockSpec(memory_space=pltpu.HBM)] * 3,
        out_specs=(pl.BlockSpec(memory_space=pltpu.VMEM), pl.BlockSpec(memory_space=pltpu.VMEM)),
        scratch_shapes=[
            pltpu.VMEM((ROWS, LANES), F32),
            pltpu.VMEM((ROWS, LANES), F32),
            pltpu.VMEM((PIECE, LANES), F32),
            pltpu.VMEM((SLOTS, 2 * PIECE, LANES), BF16),
            pltpu.VMEM((SLOTS, 2 * PIECE, LANES), BF16),
            pltpu.VMEM((SLOTS, 2 * PIECE, LANES), BF16),
            pltpu.VMEM((SLOTS, 2 * PIECE, LANES), BF16),
            pltpu.VMEM((VECS * STRIDE, LANES), F32),
            pltpu.VMEM((VECS, LANES), F32),
            pltpu.VMEM((2, 8, LANES), F32),
            pltpu.VMEM((len(PLANE) + 1, 8, LANES), F32),
            pltpu.VMEM((len(RING_SUM) + 1, 8, LANES), F32),
            dma((2, CHIPS)),
            dma((1,)),
            dma((HI_PARTS,)),
            dma((HI_PARTS, SLOTS)),
            *[dma((LO_PARTS,))] * 2,
            *[dma((1,))] * 4,
            dma((PARTS,)),
            dma((PARTS, CHIPS)),
            *[dma((PARTS,))] * 2,
        ],
        compiler_params=pltpu.CompilerParams(
            collective_id=0, has_side_effects=True, vmem_limit_bytes=VMEM_LIMIT
        ),
        name="lbfgs",
    )(step, diff, grad)


def write(direction_v, gram_v, direction_hbm, gram_hbm, sem):
    copies = [pltpu.make_async_copy(gram_v, gram_hbm, sem.at[STORES])]
    for i in range(STORES):
        rows = pl.ds(i * ROWS // STORES, ROWS // STORES)
        copies.append(pltpu.make_async_copy(direction_v.at[rows], direction_hbm.at[rows], sem.at[i]))
    for copy in copies:
        copy.start()
    for copy in copies:
        copy.wait()


def store(direction, gram):
    return pl.pallas_call(
        write,
        out_shape=(
            jax.ShapeDtypeStruct(direction.shape, F32),
            jax.ShapeDtypeStruct(gram.shape, F32),
        ),
        in_specs=[pl.BlockSpec(memory_space=pltpu.VMEM)] * 2,
        out_specs=(pl.BlockSpec(memory_space=pl.ANY), pl.BlockSpec(memory_space=pl.ANY)),
        scratch_shapes=[pltpu.SemaphoreType.DMA((STORES + 1,))],
        compiler_params=pltpu.CompilerParams(vmem_limit_bytes=2**20),
        name="store",
    )(direction, gram)


def shards(step_hist, diff_hist, gradient):
    shape = (ROWS, LANES)
    direction, gram = store(*call(step_hist.reshape(shape), diff_hist.reshape(shape), gradient.reshape(shape)))
    return direction.reshape(ROWS * LANES), gram


def solution(mesh):
    in_specs = (P("slot", "param"), P("slot", "param"), P("param"))
    out_specs = (P("param"), P())
    return jax.shard_map(shards, mesh=mesh, in_specs=in_specs, out_specs=out_specs, check_vma=False)
```

```python
import functools

import jax
import jax.numpy as jnp
from jax import lax
from jax.experimental import pallas as pl
from jax.experimental.pallas import tpu as pltpu
from jax.sharding import PartitionSpec as P

HIST = 16
SLOTS = 16
COLS = 16
ROWS = 1024
PIECE = ROWS // SLOTS
VECS = 40
LANES = 128
STRIDE = PIECE + 8
F32, BF16 = jnp.float32, jnp.bfloat16
MESH = pl.DeviceIdType.MESH
SIDE = 4
CHIPS = SLOTS // 2
STORES = 1
VMEM_LIMIT = 56 * 2**20
LOADS_FIRST = 0
RING_FIRST = True
CORES_IN_PLANE = False
TILE = 16
HI_PARTS = 1
SPAN = PIECE // HI_PARTS
CUTS = (0, 16, 64)
LO_CUTS = (0, 32, 128)
LO_EARLY = 1
PARTS = len(CUTS) - 1
LO_PARTS = len(LO_CUTS) - 1


def hops(offset, around):
    return min(offset, around - offset)


HOPS = (4, 3, 5, 2, 6, 1, 7, 0)
RING = [(dz, flip) for dz in HOPS for flip in (0, 1) if dz or flip]
RING_SUM = [(dz, flip) for dz, flip in RING if not (CORES_IN_PLANE and (flip or not dz))]
ORDER = (0, 4, 1, 5, 2, 6, 3, 7)
PASS = (4, 3, 5, 2, 6, 1, 7)
PLANE = sorted(
    ((x, y, flip) for x in range(SIDE) for y in range(SIDE) for flip in range(1 + CORES_IN_PLANE) if x or y or flip),
    key=lambda o: (-hops(o[0], SIDE) - hops(o[1], SIDE), o),
)
STARTS = (0, 40, 72, 96, 112)


def lanes_between(low, high):
    lane = lax.broadcasted_iota(jnp.int32, (8, LANES), 1)
    return jnp.logical_and(lane >= low, lane < high)


def pack(matrix):
    packed = jnp.zeros((8, LANES), F32)
    for block in range(5):
        rows = matrix[8 * block : 8 * block + 8, :]
        shift = STARTS[block] - 8 * block
        if shift:
            rows = pltpu.roll(rows, shift, 1)
        packed = jnp.where(lanes_between(STARTS[block], STARTS[block] + 40 - 8 * block), rows, packed)
    return packed


def unpack(packed):
    blocks = []
    for block in range(5):
        shift = STARTS[block] - 8 * block
        rows = pltpu.roll(packed, LANES - shift, 1) if shift else packed
        blocks.append(jnp.where(lanes_between(8 * block, 40), rows, 0.0))
    upper = jnp.concatenate(blocks, axis=0)
    lower = jnp.transpose(upper)[:VECS, :]
    lower = jnp.concatenate([lower, jnp.zeros((VECS, LANES - VECS), F32)], axis=1)
    row = lax.broadcasted_iota(jnp.int32, (VECS, LANES), 0)
    col = lax.broadcasted_iota(jnp.int32, (VECS, LANES), 1)
    return jnp.where(col // 8 >= row // 8, upper, lower)


def recursion(gram):
    row = lax.broadcasted_iota(jnp.int32, (VECS, LANES), 0)
    col = lax.broadcasted_iota(jnp.int32, (VECS, LANES), 1)

    def column(j):
        return jnp.broadcast_to(gram[:, j : j + 1], (VECS, LANES))

    def spread(value, i):
        return jnp.broadcast_to(value[i : i + 1, :], (8, LANES))

    def tall(tile):
        return jnp.concatenate([tile] * (VECS // 8), axis=0)

    pairs = jnp.sum(jnp.where(col == row + HIST, gram, 0.0), axis=1, keepdims=True)
    inverses = 1.0 / jnp.broadcast_to(pairs, (VECS, LANES))
    inverse = [spread(inverses, i) for i in range(HIST)]
    products = -column(2 * HIST)
    alphas, steps, diffs = [None] * HIST, [None] * HIST, [None] * HIST
    for i in reversed(range(HIST)):
        alphas[i] = inverse[i] * spread(products, i)
        products = products - tall(alphas[i]) * column(HIST + i)
    scale = spread(column(2 * HIST - 1), HIST - 1) / spread(column(2 * HIST - 1), 2 * HIST - 1)
    products = products * tall(scale)
    for i in range(HIST):
        steps[i] = alphas[i] - inverse[i] * spread(products, HIST + i)
        products = products + tall(steps[i]) * column(i)
        diffs[i] = -alphas[i] * scale
    return steps, diffs, -scale


def kernel(
    step_hbm, diff_hbm, grad_hbm, out_ref, gram_ref,
    step_v, diff_v, grad_v, hi_send, lo_send, hi_recv, lo_recv, wide, square, staged, plane_parts, ring_parts,
    load_sem, grad_sem, hi_ss, hi_rs, lo_ss, lo_rs, plane_ss, plane_rs, ring_ss, ring_rs, dir_ss, dir_rs, pass_ss, pass_rs,
):
    me = lax.axis_index("slot")
    col = lax.axis_index("param")
    mate = me + 1 - 2 * lax.rem(me, 2)
    chip, core = me // 2, lax.rem(me, 2)
    own_rows = pl.ds(pl.multiple_of(me * PIECE, PIECE), PIECE)

    def across(dx, dy, flip):
        x, y = col // SIDE, lax.rem(col, SIDE)
        peer = {"param": lax.rem(x + dx, SIDE) * SIDE + lax.rem(y + dy, SIDE)}
        return {**peer, "slot": mate} if flip else peer

    def along(dz, flip):
        return lax.rem(chip + dz, CHIPS) * 2 + (1 - core if flip else core)

    def load(dz):
        rows = pl.ds(pl.multiple_of(lax.rem(chip + dz, CHIPS) * 2 * PIECE, 2 * PIECE), 2 * PIECE)
        return [
            pltpu.make_async_copy(source.at[rows], target.at[rows], load_sem.at[i, dz])
            for i, (source, target) in enumerate(((step_hbm, step_v), (diff_hbm, diff_v)))
        ]

    loads = {dz: load(dz) for dz in HOPS}
    grad_load = pltpu.make_async_copy(grad_hbm.at[own_rows], grad_v, grad_sem.at[0])
    for dz in HOPS[:LOADS_FIRST]:
        for copy in loads[dz]:
            copy.start()
    barrier = pltpu.get_barrier_semaphore()
    peers = [{"slot": along(dz, flip)} for dz, flip in RING]
    peers += [across(dx, dy, flip) for dx, dy, flip in PLANE]
    for peer in peers:
        pl.semaphore_signal(barrier, inc=1, device_id=peer, device_id_type=MESH)
    for dz in HOPS[LOADS_FIRST:]:
        for copy in loads[dz]:
            copy.start()
    grad_load.start()
    pl.semaphore_wait(barrier, len(peers))
    hi_copies = []
    for part in range(HI_PARTS):
        rows = pl.ds(2 * SPAN * part, 2 * SPAN)
        for i, (dz, flip) in enumerate(RING):
            if not part and (not flip or not dz):
                for copy in loads[dz]:
                    copy.wait()
            dest = along(dz, flip)
            for half, source in ((0, step_v), (SPAN, diff_v)):
                v = source[pl.ds(pl.multiple_of(dest * PIECE + part * SPAN, 8), SPAN), :]
                at = 2 * SPAN * part + half
                hi_send[dest, at : at + SPAN, :] = v.astype(BF16)
            copy = pltpu.make_async_remote_copy(
                hi_send.at[dest, rows], hi_recv.at[me, rows], hi_ss.at[part], hi_rs.at[part, i],
                device_id={"slot": dest}, device_id_type=MESH,
            )
            copy.start()
            hi_copies.append(copy)
        for half, source in ((0, step_v), (SPAN, diff_v)):
            v = source[pl.ds(pl.multiple_of(me * PIECE + part * SPAN, 8), SPAN), :]
            at = 2 * SPAN * part + half
            hi_recv[me, at : at + SPAN, :] = v.astype(BF16)

    for k in range(SLOTS):
        for half, source in ((0, step_v), (TILE, diff_v)):
            for row in range(0, PIECE, TILE):
                v = source[k * PIECE + row : k * PIECE + row + TILE, :]
                lo_send[k, 2 * row + half : 2 * row + half + TILE, :] = (v - v.astype(BF16).astype(F32)).astype(BF16)

    def together(ref, send_sem, recv_sem):
        return pltpu.make_async_remote_copy(
            ref, ref, send_sem, recv_sem, device_id={"slot": mate}, device_id_type=MESH
        )

    def send_lo(part):
        rows = pl.ds(LO_CUTS[part], LO_CUTS[part + 1] - LO_CUTS[part])
        for offset in RING:
            dest = along(*offset)
            pltpu.make_async_remote_copy(
                lo_send.at[dest, rows], lo_recv.at[me, rows], lo_ss.at[part], lo_rs.at[part],
                device_id={"slot": dest}, device_id_type=MESH,
            ).start()
        return together(lo_recv.at[pl.ds(0, len(RING)), rows], lo_ss.at[part], lo_rs.at[part])

    for part in range(HI_PARTS):
        rows = pl.ds(2 * SPAN * part, 2 * SPAN)
        together(hi_recv.at[pl.ds(0, len(RING)), rows], hi_ss.at[part], hi_rs.at[part, 0]).wait_send()
    lo_copies = [send_lo(part) for part in range(LO_EARLY)]
    lo_recv[me] = lo_send[me]
    grad_load.wait()
    wide[2 * HIST * STRIDE : 2 * HIST * STRIDE + PIECE, :] = grad_v[...].astype(BF16).astype(F32)
    for j in range(2 * HIST + 1, VECS):
        wide[j * STRIDE : j * STRIDE + PIECE, :] = jnp.zeros((PIECE, LANES), F32)

    def widen(k, part):
        at = 2 * SPAN * part
        for j, row in ((k, at), (HIST + k, at + SPAN)):
            rows = pl.ds(pl.multiple_of(j * STRIDE + part * SPAN, 8), SPAN)
            wide[rows, :] = hi_recv[k, row : row + SPAN, :].astype(F32)

    products = jnp.zeros((VECS, VECS), F32)
    for part in range(HI_PARTS):
        widen(me, part)
        for i, (dz, flip) in enumerate(RING):
            hi_copies[part * len(RING) + i].wait_recv()
            widen(along(CHIPS - dz, flip), part)
        rows = [wide[pl.ds(r, VECS, stride=STRIDE), :].astype(BF16) for r in range(part * SPAN, (part + 1) * SPAN)]
        flat = jnp.concatenate(rows, axis=1)
        products = products + lax.dot_general(flat, flat, (((1,), (1,)), ((), ())), preferred_element_type=F32)
    square[...] = jnp.zeros((VECS, LANES), F32)
    square[:, :VECS] = products
    packed = pack(square[...])

    def exchange(value, number, parts, mine, peers, send_sems, recv_sems):
        staged[number] = value
        parts[mine] = value
        for peer in peers:
            pltpu.make_async_remote_copy(
                staged.at[number], parts.at[mine], send_sems.at[0], recv_sems.at[0],
                device_id=peer, device_id_type=MESH,
            ).start()
        return together(parts.at[pl.ds(0, len(peers))], send_sems.at[0], recv_sems.at[0])

    def total(parts):
        values = [parts[k] for k in range(parts.shape[0])]
        while len(values) > 1:
            values = [a + b for a, b in zip(values[::2], values[1::2])]
        return values[0]

    plane_mine = col + COLS * core if CORES_IN_PLANE else col
    ring_mine = chip if CORES_IN_PLANE else me
    ring_peers = [{"slot": along(*offset)} for offset in RING_SUM]
    plane_peers = [across(*offset) for offset in PLANE]
    stages = [(ring_parts, ring_mine, ring_peers, ring_ss, ring_rs), (plane_parts, plane_mine, plane_peers, plane_ss, plane_rs)]
    if not RING_FIRST:
        stages.reverse()
    copies = exchange(packed, 0, *stages[0])
    if RING_FIRST:
        lo_copies += [send_lo(part) for part in range(LO_EARLY, LO_PARTS)]
    copies.wait_recv()
    first = copies
    copies = exchange(total(stages[0][0]), 1, *stages[1])
    first.wait_send()
    if not RING_FIRST:
        lo_copies += [send_lo(part) for part in range(LO_EARLY, LO_PARTS)]
    copies.wait_recv()
    gram = unpack(total(stages[1][0]) * (1.0 / (ROWS * LANES * COLS)))
    gram_ref[...] = gram[: 2 * HIST + 1, : 2 * HIST + 1]
    steps, diffs, grad_coeff = recursion(gram)

    def piece(slot, part):
        start = pl.multiple_of(slot * PIECE + CUTS[part], 8)
        return out_ref.at[pl.ds(start, CUTS[part + 1] - CUTS[part])]

    steps, diffs = ([jnp.concatenate([c, c], axis=0) for c in side] for side in (steps, diffs))
    grad_coeff = jnp.concatenate([grad_coeff, grad_coeff], axis=0)

    def combine(at, source, span, acc):
        for k in range(SLOTS):
            acc = acc + steps[k] * source[k, at : at + TILE, :].astype(F32)
            acc = acc + diffs[k] * source[k, at + span : at + span + TILE, :].astype(F32)
        return acc

    def send_piece(k, n):
        copy = pltpu.make_async_remote_copy(
            piece(me, n), piece(me, n), dir_ss.at[n], dir_rs.at[n, chip],
            device_id={"slot": 2 * k + core}, device_id_type=MESH,
        )
        pl.when(chip != k)(copy.start)

    def pass_on(source, n):
        pltpu.make_async_remote_copy(
            piece(source, n), piece(source, n), pass_ss.at[n], pass_rs.at[n],
            device_id={"slot": mate}, device_id_type=MESH,
        ).start()

    def pieces(number, n):
        return out_ref.at[pl.ds(0, number * (CUTS[n + 1] - CUTS[n]))]

    sums = {}
    for low in range(0, PIECE, TILE):
        at = low // SPAN * 2 * SPAN + low % SPAN
        sums[low] = combine(at, hi_recv, SPAN, grad_coeff * grad_v[low : low + TILE, :])
    for n in range(PARTS):
        arrived = sum(low < 2 * CUTS[n] for low in LO_CUTS[:-1]) if n else 0
        needed = sum(low < 2 * CUTS[n + 1] for low in LO_CUTS[:-1])
        for part in range(arrived, needed):
            lo_copies[part].wait_recv()
        for low in range(CUTS[n], CUTS[n + 1], TILE):
            out_ref[pl.ds(pl.multiple_of(me * PIECE + low, TILE), TILE), :] = combine(2 * low, lo_recv, TILE, sums[low])
        for k in ORDER:
            send_piece(k, n)
        pass_on(me, n)
    copies.wait_send()
    for copy in lo_copies:
        copy.wait_send()
    for n in range(PARTS):
        for dz in PASS:
            k = lax.rem(chip + CHIPS - dz, CHIPS)
            source = 2 * k + core
            together(piece(source, n), dir_ss.at[n], dir_rs.at[n, k]).wait_recv()
            pass_on(source, n)
    for n in range(PARTS):
        together(pieces(CHIPS - 1, n), dir_ss.at[n], pass_rs.at[n]).wait_send()
        together(pieces(CHIPS, n), pass_ss.at[n], pass_rs.at[n]).wait_send()
    for n in range(PARTS):
        together(pieces(CHIPS, n), pass_ss.at[n], pass_rs.at[n]).wait_recv()


def call(step, diff, grad):
    dma = pltpu.SemaphoreType.DMA
    return pl.pallas_call(
        kernel,
        out_shape=(pltpu.VMEM((ROWS, LANES), F32), pltpu.VMEM((2 * HIST + 1, 2 * HIST + 1), F32)),
        in_specs=[pl.BlockSpec(memory_space=pltpu.HBM)] * 3,
        out_specs=(pl.BlockSpec(memory_space=pltpu.VMEM), pl.BlockSpec(memory_space=pltpu.VMEM)),
        scratch_shapes=[
            pltpu.VMEM((ROWS, LANES), F32),
            pltpu.VMEM((ROWS, LANES), F32),
            pltpu.VMEM((PIECE, LANES), F32),
            pltpu.VMEM((SLOTS, 2 * PIECE, LANES), BF16),
            pltpu.VMEM((SLOTS, 2 * PIECE, LANES), BF16),
            pltpu.VMEM((SLOTS, 2 * PIECE, LANES), BF16),
            pltpu.VMEM((SLOTS, 2 * PIECE, LANES), BF16),
            pltpu.VMEM((VECS * STRIDE, LANES), F32),
            pltpu.VMEM((VECS, LANES), F32),
            pltpu.VMEM((2, 8, LANES), F32),
            pltpu.VMEM((len(PLANE) + 1, 8, LANES), F32),
            pltpu.VMEM((len(RING_SUM) + 1, 8, LANES), F32),
            dma((2, CHIPS)),
            dma((1,)),
            dma((HI_PARTS,)),
            dma((HI_PARTS, SLOTS)),
            *[dma((LO_PARTS,))] * 2,
            *[dma((1,))] * 4,
            dma((PARTS,)),
            dma((PARTS, CHIPS)),
            *[dma((PARTS,))] * 2,
        ],
        compiler_params=pltpu.CompilerParams(
            collective_id=0, has_side_effects=True, vmem_limit_bytes=VMEM_LIMIT
        ),
        name="lbfgs",
    )(step, diff, grad)


def write(direction_v, gram_v, direction_hbm, gram_hbm, sem):
    copies = [pltpu.make_async_copy(gram_v, gram_hbm, sem.at[STORES])]
    for i in range(STORES):
        rows = pl.ds(i * ROWS // STORES, ROWS // STORES)
        copies.append(pltpu.make_async_copy(direction_v.at[rows], direction_hbm.at[rows], sem.at[i]))
    for copy in copies:
        copy.start()
    for copy in copies:
        copy.wait()


def store(direction, gram):
    return pl.pallas_call(
        write,
        out_shape=(
            jax.ShapeDtypeStruct(direction.shape, F32),
            jax.ShapeDtypeStruct(gram.shape, F32),
        ),
        in_specs=[pl.BlockSpec(memory_space=pltpu.VMEM)] * 2,
        out_specs=(pl.BlockSpec(memory_space=pl.ANY), pl.BlockSpec(memory_space=pl.ANY)),
        scratch_shapes=[pltpu.SemaphoreType.DMA((STORES + 1,))],
        compiler_params=pltpu.CompilerParams(vmem_limit_bytes=2**20),
        name="store",
    )(direction, gram)


def shards(step_hist, diff_hist, gradient):
    shape = (ROWS, LANES)
    direction, gram = store(*call(step_hist.reshape(shape), diff_hist.reshape(shape), gradient.reshape(shape)))
    return direction.reshape(ROWS * LANES), gram


def solution(mesh):
    in_specs = (P("slot", "param"), P("slot", "param"), P("param"))
    out_specs = (P("param"), P())
    return jax.shard_map(shards, mesh=mesh, in_specs=in_specs, out_specs=out_specs, check_vma=False)
```

```python
import functools

import jax
import jax.numpy as jnp
from jax import lax
from jax.experimental import pallas as pl
from jax.experimental.pallas import tpu as pltpu
from jax.sharding import PartitionSpec as P

HIST = 16
SLOTS = 16
COLS = 16
ROWS = 1024
PIECE = ROWS // SLOTS
VECS = 40
LANES = 128
STRIDE = PIECE + 8
F32, BF16 = jnp.float32, jnp.bfloat16
MESH = pl.DeviceIdType.MESH
SIDE = 4
CHIPS = SLOTS // 2
STORES = 1
VMEM_LIMIT = 56 * 2**20
LOADS_FIRST = 0
RING_FIRST = True
CORES_IN_PLANE = False
TILE = 16
HI_PARTS = 1
SPAN = PIECE // HI_PARTS
CUTS = (0, 32, 64)
LO_CUTS = (0, 32, 64, 128)
LO_EARLY = 1
PARTS = len(CUTS) - 1
LO_PARTS = len(LO_CUTS) - 1


def hops(offset, around):
    return min(offset, around - offset)


HOPS = (4, 3, 5, 2, 6, 1, 7, 0)
RING = [(dz, flip) for dz in HOPS for flip in (0, 1) if dz or flip]
RING_SUM = [(dz, flip) for dz, flip in RING if not (CORES_IN_PLANE and (flip or not dz))]
ORDER = (0, 4, 1, 5, 2, 6, 3, 7)
PASS = (1, 7, 2, 6, 3, 5, 4)
PLANE = sorted(
    ((x, y, flip) for x in range(SIDE) for y in range(SIDE) for flip in range(1 + CORES_IN_PLANE) if x or y or flip),
    key=lambda o: (-hops(o[0], SIDE) - hops(o[1], SIDE), o),
)
STARTS = (0, 40, 72, 96, 112)


def lanes_between(low, high):
    lane = lax.broadcasted_iota(jnp.int32, (8, LANES), 1)
    return jnp.logical_and(lane >= low, lane < high)


def pack(matrix):
    packed = jnp.zeros((8, LANES), F32)
    for block in range(5):
        rows = matrix[8 * block : 8 * block + 8, :]
        shift = STARTS[block] - 8 * block
        if shift:
            rows = pltpu.roll(rows, shift, 1)
        packed = jnp.where(lanes_between(STARTS[block], STARTS[block] + 40 - 8 * block), rows, packed)
    return packed


def unpack(packed):
    blocks = []
    for block in range(5):
        shift = STARTS[block] - 8 * block
        rows = pltpu.roll(packed, LANES - shift, 1) if shift else packed
        blocks.append(jnp.where(lanes_between(8 * block, 40), rows, 0.0))
    upper = jnp.concatenate(blocks, axis=0)
    lower = jnp.transpose(upper)[:VECS, :]
    lower = jnp.concatenate([lower, jnp.zeros((VECS, LANES - VECS), F32)], axis=1)
    row = lax.broadcasted_iota(jnp.int32, (VECS, LANES), 0)
    col = lax.broadcasted_iota(jnp.int32, (VECS, LANES), 1)
    return jnp.where(col // 8 >= row // 8, upper, lower)


def recursion(gram):
    row = lax.broadcasted_iota(jnp.int32, (VECS, LANES), 0)
    col = lax.broadcasted_iota(jnp.int32, (VECS, LANES), 1)

    def column(j):
        return jnp.broadcast_to(gram[:, j : j + 1], (VECS, LANES))

    def spread(value, i):
        return jnp.broadcast_to(value[i : i + 1, :], (8, LANES))

    def tall(tile):
        return jnp.concatenate([tile] * (VECS // 8), axis=0)

    pairs = jnp.sum(jnp.where(col == row + HIST, gram, 0.0), axis=1, keepdims=True)
    inverses = 1.0 / jnp.broadcast_to(pairs, (VECS, LANES))
    inverse = [spread(inverses, i) for i in range(HIST)]
    products = -column(2 * HIST)
    alphas, steps, diffs = [None] * HIST, [None] * HIST, [None] * HIST
    for i in reversed(range(HIST)):
        alphas[i] = inverse[i] * spread(products, i)
        products = products - tall(alphas[i]) * column(HIST + i)
    scale = spread(column(2 * HIST - 1), HIST - 1) / spread(column(2 * HIST - 1), 2 * HIST - 1)
    products = products * tall(scale)
    for i in range(HIST):
        steps[i] = alphas[i] - inverse[i] * spread(products, HIST + i)
        products = products + tall(steps[i]) * column(i)
        diffs[i] = -alphas[i] * scale
    return steps, diffs, -scale


def kernel(
    step_hbm, diff_hbm, grad_hbm, out_ref, gram_ref,
    step_v, diff_v, grad_v, hi_send, lo_send, hi_recv, lo_recv, wide, square, staged, plane_parts, ring_parts,
    load_sem, grad_sem, hi_ss, hi_rs, lo_ss, lo_rs, plane_ss, plane_rs, ring_ss, ring_rs, dir_ss, dir_rs, pass_ss, pass_rs,
):
    me = lax.axis_index("slot")
    col = lax.axis_index("param")
    mate = me + 1 - 2 * lax.rem(me, 2)
    chip, core = me // 2, lax.rem(me, 2)
    own_rows = pl.ds(pl.multiple_of(me * PIECE, PIECE), PIECE)

    def across(dx, dy, flip):
        x, y = col // SIDE, lax.rem(col, SIDE)
        peer = {"param": lax.rem(x + dx, SIDE) * SIDE + lax.rem(y + dy, SIDE)}
        return {**peer, "slot": mate} if flip else peer

    def along(dz, flip):
        return lax.rem(chip + dz, CHIPS) * 2 + (1 - core if flip else core)

    def load(dz):
        rows = pl.ds(pl.multiple_of(lax.rem(chip + dz, CHIPS) * 2 * PIECE, 2 * PIECE), 2 * PIECE)
        return [
            pltpu.make_async_copy(source.at[rows], target.at[rows], load_sem.at[i, dz])
            for i, (source, target) in enumerate(((step_hbm, step_v), (diff_hbm, diff_v)))
        ]

    loads = {dz: load(dz) for dz in HOPS}
    grad_load = pltpu.make_async_copy(grad_hbm.at[own_rows], grad_v, grad_sem.at[0])
    for dz in HOPS[:LOADS_FIRST]:
        for copy in loads[dz]:
            copy.start()
    barrier = pltpu.get_barrier_semaphore()
    peers = [{"slot": along(dz, flip)} for dz, flip in RING]
    peers += [across(dx, dy, flip) for dx, dy, flip in PLANE]
    for peer in peers:
        pl.semaphore_signal(barrier, inc=1, device_id=peer, device_id_type=MESH)
    for dz in HOPS[LOADS_FIRST:]:
        for copy in loads[dz]:
            copy.start()
    grad_load.start()
    pl.semaphore_wait(barrier, len(peers))
    hi_copies = []
    for part in range(HI_PARTS):
        rows = pl.ds(2 * SPAN * part, 2 * SPAN)
        for i, (dz, flip) in enumerate(RING):
            if not part and (not flip or not dz):
                for copy in loads[dz]:
                    copy.wait()
            dest = along(dz, flip)
            for half, source in ((0, step_v), (SPAN, diff_v)):
                v = source[pl.ds(pl.multiple_of(dest * PIECE + part * SPAN, 8), SPAN), :]
                at = 2 * SPAN * part + half
                hi_send[dest, at : at + SPAN, :] = v.astype(BF16)
            copy = pltpu.make_async_remote_copy(
                hi_send.at[dest, rows], hi_recv.at[me, rows], hi_ss.at[part], hi_rs.at[part, i],
                device_id={"slot": dest}, device_id_type=MESH,
            )
            copy.start()
            hi_copies.append(copy)
        for half, source in ((0, step_v), (SPAN, diff_v)):
            v = source[pl.ds(pl.multiple_of(me * PIECE + part * SPAN, 8), SPAN), :]
            at = 2 * SPAN * part + half
            hi_recv[me, at : at + SPAN, :] = v.astype(BF16)

    for k in range(SLOTS):
        for half, source in ((0, step_v), (TILE, diff_v)):
            for row in range(0, PIECE, TILE):
                v = source[k * PIECE + row : k * PIECE + row + TILE, :]
                lo_send[k, 2 * row + half : 2 * row + half + TILE, :] = (v - v.astype(BF16).astype(F32)).astype(BF16)

    def together(ref, send_sem, recv_sem):
        return pltpu.make_async_remote_copy(
            ref, ref, send_sem, recv_sem, device_id={"slot": mate}, device_id_type=MESH
        )

    def send_lo(part):
        rows = pl.ds(LO_CUTS[part], LO_CUTS[part + 1] - LO_CUTS[part])
        for offset in RING:
            dest = along(*offset)
            pltpu.make_async_remote_copy(
                lo_send.at[dest, rows], lo_recv.at[me, rows], lo_ss.at[part], lo_rs.at[part],
                device_id={"slot": dest}, device_id_type=MESH,
            ).start()
        return together(lo_recv.at[pl.ds(0, len(RING)), rows], lo_ss.at[part], lo_rs.at[part])

    for part in range(HI_PARTS):
        rows = pl.ds(2 * SPAN * part, 2 * SPAN)
        together(hi_recv.at[pl.ds(0, len(RING)), rows], hi_ss.at[part], hi_rs.at[part, 0]).wait_send()
    lo_copies = [send_lo(part) for part in range(LO_EARLY)]
    lo_recv[me] = lo_send[me]
    grad_load.wait()
    wide[2 * HIST * STRIDE : 2 * HIST * STRIDE + PIECE, :] = grad_v[...].astype(BF16).astype(F32)
    for j in range(2 * HIST + 1, VECS):
        wide[j * STRIDE : j * STRIDE + PIECE, :] = jnp.zeros((PIECE, LANES), F32)

    def widen(k, part):
        at = 2 * SPAN * part
        for j, row in ((k, at), (HIST + k, at + SPAN)):
            rows = pl.ds(pl.multiple_of(j * STRIDE + part * SPAN, 8), SPAN)
            wide[rows, :] = hi_recv[k, row : row + SPAN, :].astype(F32)

    products = jnp.zeros((VECS, VECS), F32)
    for part in range(HI_PARTS):
        widen(me, part)
        for i, (dz, flip) in enumerate(RING):
            hi_copies[part * len(RING) + i].wait_recv()
            widen(along(CHIPS - dz, flip), part)
        rows = [wide[pl.ds(r, VECS, stride=STRIDE), :].astype(BF16) for r in range(part * SPAN, (part + 1) * SPAN)]
        flat = jnp.concatenate(rows, axis=1)
        products = products + lax.dot_general(flat, flat, (((1,), (1,)), ((), ())), preferred_element_type=F32)
    square[...] = jnp.zeros((VECS, LANES), F32)
    square[:, :VECS] = products
    packed = pack(square[...])

    def exchange(value, number, parts, mine, peers, send_sems, recv_sems):
        staged[number] = value
        parts[mine] = value
        for peer in peers:
            pltpu.make_async_remote_copy(
                staged.at[number], parts.at[mine], send_sems.at[0], recv_sems.at[0],
                device_id=peer, device_id_type=MESH,
            ).start()
        return together(parts.at[pl.ds(0, len(peers))], send_sems.at[0], recv_sems.at[0])

    def total(parts):
        values = [parts[k] for k in range(parts.shape[0])]
        while len(values) > 1:
            values = [a + b for a, b in zip(values[::2], values[1::2])]
        return values[0]

    plane_mine = col + COLS * core if CORES_IN_PLANE else col
    ring_mine = chip if CORES_IN_PLANE else me
    ring_peers = [{"slot": along(*offset)} for offset in RING_SUM]
    plane_peers = [across(*offset) for offset in PLANE]
    stages = [(ring_parts, ring_mine, ring_peers, ring_ss, ring_rs), (plane_parts, plane_mine, plane_peers, plane_ss, plane_rs)]
    if not RING_FIRST:
        stages.reverse()
    copies = exchange(packed, 0, *stages[0])
    if RING_FIRST:
        lo_copies += [send_lo(part) for part in range(LO_EARLY, LO_PARTS)]
    copies.wait_recv()
    first = copies
    copies = exchange(total(stages[0][0]), 1, *stages[1])
    first.wait_send()
    if not RING_FIRST:
        lo_copies += [send_lo(part) for part in range(LO_EARLY, LO_PARTS)]
    copies.wait_recv()
    gram = unpack(total(stages[1][0]) * (1.0 / (ROWS * LANES * COLS)))
    gram_ref[...] = gram[: 2 * HIST + 1, : 2 * HIST + 1]
    steps, diffs, grad_coeff = recursion(gram)

    def piece(slot, part):
        start = pl.multiple_of(slot * PIECE + CUTS[part], 8)
        return out_ref.at[pl.ds(start, CUTS[part + 1] - CUTS[part])]

    steps, diffs = ([jnp.concatenate([c, c], axis=0) for c in side] for side in (steps, diffs))
    grad_coeff = jnp.concatenate([grad_coeff, grad_coeff], axis=0)

    def combine(at, source, span, acc):
        for k in range(SLOTS):
            acc = acc + steps[k] * source[k, at : at + TILE, :].astype(F32)
            acc = acc + diffs[k] * source[k, at + span : at + span + TILE, :].astype(F32)
        return acc

    def send_piece(k, n):
        copy = pltpu.make_async_remote_copy(
            piece(me, n), piece(me, n), dir_ss.at[n], dir_rs.at[n, chip],
            device_id={"slot": 2 * k + core}, device_id_type=MESH,
        )
        pl.when(chip != k)(copy.start)

    def pass_on(source, n):
        pltpu.make_async_remote_copy(
            piece(source, n), piece(source, n), pass_ss.at[n], pass_rs.at[n],
            device_id={"slot": mate}, device_id_type=MESH,
        ).start()

    def pieces(number, n):
        return out_ref.at[pl.ds(0, number * (CUTS[n + 1] - CUTS[n]))]

    sums = {}
    for low in range(0, PIECE, TILE):
        at = low // SPAN * 2 * SPAN + low % SPAN
        sums[low] = combine(at, hi_recv, SPAN, grad_coeff * grad_v[low : low + TILE, :])
    for n in range(PARTS):
        arrived = sum(low < 2 * CUTS[n] for low in LO_CUTS[:-1]) if n else 0
        needed = sum(low < 2 * CUTS[n + 1] for low in LO_CUTS[:-1])
        for part in range(arrived, needed):
            lo_copies[part].wait_recv()
        for low in range(CUTS[n], CUTS[n + 1], TILE):
            out_ref[pl.ds(pl.multiple_of(me * PIECE + low, TILE), TILE), :] = combine(2 * low, lo_recv, TILE, sums[low])
        for k in ORDER:
            send_piece(k, n)
        pass_on(me, n)
    copies.wait_send()
    for copy in lo_copies:
        copy.wait_send()
    for n in range(PARTS):
        for dz in PASS:
            k = lax.rem(chip + CHIPS - dz, CHIPS)
            source = 2 * k + core
            together(piece(source, n), dir_ss.at[n], dir_rs.at[n, k]).wait_recv()
            pass_on(source, n)
    for n in range(PARTS):
        together(pieces(CHIPS - 1, n), dir_ss.at[n], pass_rs.at[n]).wait_send()
        together(pieces(CHIPS, n), pass_ss.at[n], pass_rs.at[n]).wait_send()
    for n in range(PARTS):
        together(pieces(CHIPS, n), pass_ss.at[n], pass_rs.at[n]).wait_recv()


def call(step, diff, grad):
    dma = pltpu.SemaphoreType.DMA
    return pl.pallas_call(
        kernel,
        out_shape=(pltpu.VMEM((ROWS, LANES), F32), pltpu.VMEM((2 * HIST + 1, 2 * HIST + 1), F32)),
        in_specs=[pl.BlockSpec(memory_space=pltpu.HBM)] * 3,
        out_specs=(pl.BlockSpec(memory_space=pltpu.VMEM), pl.BlockSpec(memory_space=pltpu.VMEM)),
        scratch_shapes=[
            pltpu.VMEM((ROWS, LANES), F32),
            pltpu.VMEM((ROWS, LANES), F32),
            pltpu.VMEM((PIECE, LANES), F32),
            pltpu.VMEM((SLOTS, 2 * PIECE, LANES), BF16),
            pltpu.VMEM((SLOTS, 2 * PIECE, LANES), BF16),
            pltpu.VMEM((SLOTS, 2 * PIECE, LANES), BF16),
            pltpu.VMEM((SLOTS, 2 * PIECE, LANES), BF16),
            pltpu.VMEM((VECS * STRIDE, LANES), F32),
            pltpu.VMEM((VECS, LANES), F32),
            pltpu.VMEM((2, 8, LANES), F32),
            pltpu.VMEM((len(PLANE) + 1, 8, LANES), F32),
            pltpu.VMEM((len(RING_SUM) + 1, 8, LANES), F32),
            dma((2, CHIPS)),
            dma((1,)),
            dma((HI_PARTS,)),
            dma((HI_PARTS, SLOTS)),
            *[dma((LO_PARTS,))] * 2,
            *[dma((1,))] * 4,
            dma((PARTS,)),
            dma((PARTS, CHIPS)),
            *[dma((PARTS,))] * 2,
        ],
        compiler_params=pltpu.CompilerParams(
            collective_id=0, has_side_effects=True, vmem_limit_bytes=VMEM_LIMIT
        ),
        name="lbfgs",
    )(step, diff, grad)


def write(direction_v, gram_v, direction_hbm, gram_hbm, sem):
    copies = [pltpu.make_async_copy(gram_v, gram_hbm, sem.at[STORES])]
    for i in range(STORES):
        rows = pl.ds(i * ROWS // STORES, ROWS // STORES)
        copies.append(pltpu.make_async_copy(direction_v.at[rows], direction_hbm.at[rows], sem.at[i]))
    for copy in copies:
        copy.start()
    for copy in copies:
        copy.wait()


def store(direction, gram):
    return pl.pallas_call(
        write,
        out_shape=(
            jax.ShapeDtypeStruct(direction.shape, F32),
            jax.ShapeDtypeStruct(gram.shape, F32),
        ),
        in_specs=[pl.BlockSpec(memory_space=pltpu.VMEM)] * 2,
        out_specs=(pl.BlockSpec(memory_space=pl.ANY), pl.BlockSpec(memory_space=pl.ANY)),
        scratch_shapes=[pltpu.SemaphoreType.DMA((STORES + 1,))],
        compiler_params=pltpu.CompilerParams(vmem_limit_bytes=2**20),
        name="store",
    )(direction, gram)


def shards(step_hist, diff_hist, gradient):
    shape = (ROWS, LANES)
    direction, gram = store(*call(step_hist.reshape(shape), diff_hist.reshape(shape), gradient.reshape(shape)))
    return direction.reshape(ROWS * LANES), gram


def solution(mesh):
    in_specs = (P("slot", "param"), P("slot", "param"), P("param"))
    out_specs = (P("param"), P())
    return jax.shard_map(shards, mesh=mesh, in_specs=in_specs, out_specs=out_specs, check_vma=False)
```
